32 devices in a mesh: fsdp: 2 (over y), ctx: 4 (over z), tp: 4 (over x, core).
Axes of the slice: x: 2, y: 2, z: 4, core: 2. Of those that a mesh axis runs over, the one named last changes fastest.
Arguments:
- tokens: bfloat16 [6, 1024, 2048], P('fsdp', 'ctx', 'tp'), may hold values from -33 to 33
- segment_ids: int32 [6, 1024], P('fsdp', 'ctx'), may hold values from 1 to 128, as said below
- positions: int32 [6, 1024], P('fsdp', 'ctx'), may hold values from 0 to 1023, as said below
- attn_gain: float32 [2048], P('tp'), may hold values from 0.1 to 1.9
- w_query: bfloat16 [2048, 2048], P('fsdp', 'tp'), may hold values from -0.125 to 0.125
- w_key: bfloat16 [2048, 512], P('fsdp', 'tp'), may hold values from -0.125 to 0.125
- w_value: bfloat16 [2048, 512], P('fsdp', 'tp'), may hold values from -0.125 to 0.125
- w_output: bfloat16 [2048, 2048], P('tp', 'fsdp'), may hold values from -0.5 to 0.5
- mlp_gain: float32 [2048], P('tp'), may hold values from 0.1 to 1.9
- w_gate: bfloat16 [2048, 8192], P('fsdp', 'tp'), may hold values from -0.125 to 0.125
- w_up: bfloat16 [2048, 8192], P('fsdp', 'tp'), may hold values from -0.125 to 0.125
- w_down: bfloat16 [8192, 2048], P('tp', 'fsdp'), may hold values from -0.0625 to 0.0625
- cotangent: bfloat16 [6, 1024, 2048], P('fsdp', 'ctx', 'tp'), may hold values from -6 to 6
Outputs:
- output: bfloat16 [6, 1024, 2048], P('fsdp', 'ctx', 'tp')
- input_grad: float32 [6, 1024, 2048], P('fsdp', 'ctx', 'tp')
- attn_gain_grad: float32 [2048], P('tp')
- w_query_grad: float32 [2048, 2048], P('fsdp', 'tp')
- w_key_grad: float32 [2048, 512], P('fsdp', 'tp')
- w_value_grad: float32 [2048, 512], P('fsdp', 'tp')
- w_output_grad: float32 [2048, 2048], P('tp', 'fsdp')
- mlp_gain_grad: float32 [2048], P('tp')
- w_gate_grad: float32 [2048, 8192], P('fsdp', 'tp')
- w_up_grad: float32 [2048, 8192], P('fsdp', 'tp')
- w_down_grad: float32 [8192, 2048], P('tp', 'fsdp')
The draws below stay inside these ranges and needn't reach their ends.
Inputs may be any that keep to these rules, and one draw needn't show every extreme that they name: `segment_ids`: within each sequence the ids start at 1, never fall and change only where a new document begins; every document but a sequence's last has 8 tokens or more, and in every group of 3 sequences one sequence is a single document and one is made of eight-token documents. `positions`: 0 where a sequence or a document begins, else one more than at the token before within its document.
All inputs are finite; a program needn't handle non-finite values.
Results may differ from the reference program's by a relative error of at most 0.013.
Values may be sent and summed in bfloat16 or wider, within the bound.
No kernel may reach another device: no remote copies, remote signals or barrier semaphores. Data moves between devices by JAX's collectives and lax.ppermute only.
A program may use at most 256 MiB of HBM per device.

```python
import math
import jax
import jax.numpy as jnp
from jax import lax

D = 2048
HQ = 32
KV = 8
HD = 64
FF = 8192
LEN = 1024
SEQS = 3
SEQ_ALL = 6
N_FSDP = 2


def documents(key):
    key_len, key_pick, key_extra, key_short = jax.random.split(key, 4)
    most_docs = LEN // 8
    top_exp = int(math.log2(LEN) + 0.5)
    exponent = jax.random.randint(key_len, (SEQ_ALL, most_docs), 3, top_exp + 1)
    spans = jnp.left_shift(jnp.ones_like(exponent), exponent)
    spans = spans + jax.random.randint(key_extra, (SEQ_ALL, most_docs), 0, 8)
    ends = jnp.cumsum(spans, axis=1)
    starts = ends - spans
    places = jnp.arange(LEN, dtype=jnp.int32)
    seg_ids = jnp.sum((ends[:, None, :] <= places[None, :, None]).astype(jnp.int32), axis=-1)
    begins = jnp.max(jnp.where(starts[:, None, :] <= places[None, :, None], starts[:, None, :], 0), axis=-1)
    offsets = places[None, :] - begins
    chosen = jax.random.randint(key_pick, (N_FSDP,), 0, SEQS)
    step_on = jax.random.randint(key_short, (N_FSDP,), 1, SEQS)
    short_pick = (chosen + step_on) % SEQS
    seq_index = jnp.arange(SEQ_ALL, dtype=jnp.int32)
    whole = seq_index % SEQS == jnp.repeat(chosen, SEQS)
    short = seq_index % SEQS == jnp.repeat(short_pick, SEQS)
    seg_ids = jnp.where(whole[:, None], 0, seg_ids)
    offsets = jnp.where(whole[:, None], places[None, :], offsets)
    seg_ids = jnp.where(short[:, None], places[None, :] // 8, seg_ids)
    offsets = jnp.where(short[:, None], places[None, :] % 8, offsets)
    return ((seg_ids + 1).astype(jnp.int32), offsets.astype(jnp.int32))


def draw_segment_ids(key, part):
    shared = documents(key)
    return shared[0]


def draw_positions(key, part):
    shared = documents(key)
    return shared[1]


def draw_tokens(key, part):
    key = jax.random.fold_in(key, 7)
    key_base, key_row = jax.random.split(key)
    feature = jnp.arange(D, dtype=jnp.float32) / (D - 1)
    seq_frac = jnp.arange(SEQ_ALL, dtype=jnp.float32) / max(SEQ_ALL - 1, 1)
    pos_frac = jnp.arange(LEN, dtype=jnp.float32) / (LEN - 1)
    rising = 0.6 * 3.0 ** ((seq_frac[:, None] + pos_frac[None, :]) / 2.0)
    row_rand = jnp.exp(jax.random.uniform(key_row, (SEQ_ALL, LEN), minval=math.log(0.25), maxval=math.log(2.5)))
    base = jnp.clip(jax.random.normal(key_base, (SEQ_ALL, LEN, D)), -4.0, 4.0)
    column = 0.6 * 3.0 ** feature
    return (base * (row_rand * rising)[..., None] * column).astype(jnp.bfloat16)


def steps_of(own_key, shape, shards, smallest, high):
    factor_of = 1.0
    for axis_at, blocks in shards:
        heights = jax.random.uniform(jax.random.fold_in(jax.random.fold_in(own_key, 6), axis_at), (blocks,), jnp.float32, smallest / len(shards), high / len(shards))
        factor_of = factor_of * jnp.repeat(jnp.exp(heights), shape[axis_at] // blocks).reshape((-1,) + (1,) * (len(shape) - 1 - axis_at))
    return factor_of


def noise(stream_key, extent, scale, limit, cuts=(), kind=jnp.bfloat16):
    factor_of = steps_of(stream_key, extent, cuts, -0.22, 0.18) if cuts else 1.0
    drawn = jax.random.normal(stream_key, extent, jnp.float32) * scale * factor_of
    return jnp.minimum(jnp.maximum(drawn, -limit), limit).astype(kind)


def setup_inputs(seed: int = 0) -> dict:
    splits = jax.random.split(jax.random.key(seed), 14)
    return {
        "tokens": draw_tokens(jax.random.fold_in(splits[13], 71), 0),
        "segment_ids": draw_segment_ids(jax.random.fold_in(splits[13], 71), 0),
        "positions": draw_positions(jax.random.fold_in(splits[13], 71), 0),
        "attn_gain": jnp.clip(1.0 + 0.18 * jax.random.normal(splits[3], (D,), jnp.float32), 0.1, 1.9),
        "w_query": noise(splits[4], (D, HQ * HD), D ** -0.5, 0.125, ((0, 2), (1, 4))),
        "w_key": noise(splits[5], (D, KV * HD), D ** -0.5, 0.125, ((0, 2), (1, 4))),
        "w_value": noise(splits[6], (D, KV * HD), D ** -0.5, 0.125, ((0, 2), (1, 4))),
        "w_output": noise(splits[7], (HQ * HD, D), (HQ * HD // 16) ** -0.5, 0.5, ((0, 4), (1, 2))),
        "mlp_gain": jnp.clip(1.0 + 0.18 * jax.random.normal(splits[8], (D,), jnp.float32), 0.1, 1.9),
        "w_gate": noise(splits[9], (D, FF), D ** -0.5, 0.125, ((0, 2), (1, 4))),
        "w_up": noise(splits[10], (D, FF), D ** -0.5, 0.125, ((0, 2), (1, 4))),
        "w_down": noise(splits[11], (FF, D), FF ** -0.5, 0.0625, ((0, 4), (1, 2))),
        "cotangent": noise(splits[12], (SEQ_ALL, LEN, D), 1.0, 6.0, ((0, 2), (1, 4), (2, 4))),
    }


THETA = 500000.0
EPS = 1e-05
NEG = -1e+30
HIGH = lax.Precision.HIGHEST

@jax.custom_vjp
def low(v):
    return lax.optimization_barrier(v.astype(jnp.bfloat16)).astype(jnp.float32)

@jax.custom_vjp
def low_back(v):
    return v

def low_keep(v):
    return (low(v), None)

def low_pass(kept, grad):
    return (grad,)

def back_keep(v):
    return (v, None)

def back_low(kept, grad):
    return (low(grad),)
low.defvjp(low_keep, low_pass)
low_back.defvjp(back_keep, back_low)

def matmul(left_rows, right_rows):
    return jnp.dot(left_rows, right_rows, precision=HIGH, preferred_element_type=jnp.float32)

def rms_scale(residual):
    return lax.rsqrt(lax.optimization_barrier(jnp.mean(residual * residual, axis=-1, keepdims=True)) + EPS)

def angles(positions):
    frequency = jnp.exp(jnp.arange(HD // 2, dtype=jnp.float32) * (-2.0 * math.log(THETA) / HD))
    turn_angle = positions.astype(jnp.float32)[..., None] * frequency
    return (jnp.cos(turn_angle)[..., None, :], jnp.sin(turn_angle)[..., None, :])

def rotate(vectors, cos_part, sin_part):
    half_dim = vectors.shape[-1] // 2
    first_half = vectors[..., :half_dim]
    second_half = vectors[..., half_dim:]
    return jnp.concatenate([first_half * cos_part - second_half * sin_part, second_half * cos_part + first_half * sin_part], axis=-1)

def attend(pieces):
    queries, key_rows, values, seg_ids = pieces
    grouped = queries.reshape(LEN, KV, HQ // KV, HD)
    raw_scores = jnp.einsum('qkgd,skd->kgqs', grouped, key_rows, precision=HIGH)
    scores = low_back(raw_scores) * HD ** (-0.5)
    places = jnp.arange(LEN)
    allowed = (seg_ids[:, None] == seg_ids[None, :]) & (places[None, :] <= places[:, None])
    scores = jnp.where(allowed, scores, NEG)
    row_max = lax.optimization_barrier(jnp.max(scores, axis=-1, keepdims=True))
    exp_terms = jnp.exp(scores - row_max)
    attn_probs = low(exp_terms / lax.optimization_barrier(jnp.sum(exp_terms, axis=-1, keepdims=True)))
    mixed = jnp.einsum('kgqs,skd->qkgd', attn_probs, values, precision=HIGH)
    return mixed.reshape(LEN, HQ * HD)

def group_layer(pieces, params):
    group_tokens, group_segs, cos_part, sin_part = pieces
    attn_gain, w_query, w_key, w_value, w_output, mlp_gain, w_gate, w_up, w_down = params
    seq_count = group_tokens.shape[0]
    normed = low(group_tokens * rms_scale(group_tokens) * attn_gain).reshape(-1, D)
    query_pre = low_back(matmul(normed, w_query)).reshape(seq_count, LEN, HQ, HD)
    key_pre = low_back(matmul(normed, w_key)).reshape(seq_count, LEN, KV, HD)
    value_rows = low(low_back(matmul(normed, w_value))).reshape(seq_count, LEN, KV, HD)
    query_rot = low(rotate(query_pre, cos_part, sin_part))
    key_rot = low(rotate(key_pre, cos_part, sin_part))
    attended = lax.map(jax.checkpoint(attend), (query_rot, key_rot, value_rows, group_segs))
    attended = low(low_back(attended)).reshape(-1, HQ * HD)
    branch = low_back(matmul(attended, w_output)).reshape(seq_count, LEN, D)
    resid_mid = group_tokens + branch
    normed_mlp = low(resid_mid * rms_scale(resid_mid) * mlp_gain).reshape(-1, D)
    gate_pre = low_back(matmul(normed_mlp, w_gate))
    up_pre = low_back(matmul(normed_mlp, w_up))
    activated = low(gate_pre * jax.nn.sigmoid(gate_pre) * up_pre)
    mlp_out = low_back(matmul(activated, w_down)).reshape(seq_count, LEN, D)
    return resid_mid + mlp_out

def reference(tokens, segment_ids, positions, attn_gain, w_query, w_key, w_value, w_output, mlp_gain, w_gate, w_up, w_down, cotangent):
    per_group = math.gcd(SEQ_ALL, max(1, 4096 // LEN))
    groups = SEQ_ALL // per_group
    cos_all, sin_all = angles(positions)

    def split_groups(stacked):
        return stacked.reshape((groups, per_group) + stacked.shape[1:])

    def forward(tokens_f, attn_gain_f, query_f, key_f, value_f, output_f, mlp_gain_f, gate_f, up_f, down_f):
        params = (attn_gain_f, query_f, key_f, value_f, output_f, mlp_gain_f, gate_f, up_f, down_f)

        def one_group(pieces):
            return group_layer(pieces, params)
        result = lax.map(jax.checkpoint(one_group), (split_groups(tokens_f), split_groups(segment_ids), split_groups(cos_all), split_groups(sin_all)))
        return result.reshape(SEQ_ALL, LEN, D)
    primals = tuple((item.astype(jnp.float32) for item in (tokens, attn_gain, w_query, w_key, w_value, w_output, mlp_gain, w_gate, w_up, w_down)))
    result_out, pullback = jax.vjp(forward, *primals)
    gradients = pullback(cotangent.astype(jnp.float32))
    return (result_out.astype(jnp.bfloat16), gradients[0], gradients[1], gradients[2], gradients[3], gradients[4], gradients[5], gradients[6], gradients[7], gradients[8], gradients[9])
```

```python
import math

import jax
import jax.numpy as jnp
from jax import lax
from jax.sharding import PartitionSpec as P

HQ = 32
KV = 8
HD = 64

THETA = 500000.0
EPS = 1e-05
NEG = -1e30
BF = jnp.bfloat16
F32 = jnp.float32


def angles(positions):
    frequency = jnp.exp(jnp.arange(HD // 2, dtype=F32) * (-2.0 * math.log(THETA) / HD))
    turn_angle = positions.astype(F32)[..., None] * frequency
    return (jnp.cos(turn_angle)[..., None, :], jnp.sin(turn_angle)[..., None, :])


def rotate(vectors, cos_part, sin_part):
    half_dim = vectors.shape[-1] // 2
    first_half = vectors[..., :half_dim]
    second_half = vectors[..., half_dim:]
    return jnp.concatenate(
        [
            first_half * cos_part - second_half * sin_part,
            second_half * cos_part + first_half * sin_part,
        ],
        axis=-1,
    )


def unrotate(grad_rows, cos_part, sin_part):
    return rotate(grad_rows, cos_part, -sin_part)


def mm(left, right):
    return jnp.dot(left, right, preferred_element_type=F32)


def mm_tn(left, right):
    return lax.dot_general(left, right, (((0,), (0,)), ((), ())), preferred_element_type=F32)


def mm_nt(left, right):
    return lax.dot_general(left, right, (((1,), (1,)), ((), ())), preferred_element_type=F32)


def flip(count, bit):
    return [(i, i ^ bit) for i in range(count)]


def tensor_gather(part):
    count = lax.axis_size("tp")
    if count != 4:
        return lax.all_gather(part, "tp", axis=1, tiled=True)
    me = lax.axis_index("tp")
    far = lax.ppermute(part, "tp", flip(4, 2))
    near = lax.ppermute(part, "tp", flip(4, 1))
    far_near = lax.ppermute(far, "tp", flip(4, 1))
    odd = me % 2 == 1
    high = me >= 2
    own_pair = (jnp.where(odd, near, part), jnp.where(odd, part, near))
    far_pair = (jnp.where(odd, far_near, far), jnp.where(odd, far, far_near))
    pieces = [jnp.where(high, f, o) for o, f in zip(own_pair, far_pair)]
    pieces += [jnp.where(high, o, f) for o, f in zip(own_pair, far_pair)]
    return jnp.concatenate(pieces, axis=1)


def tensor_scatter(partial):
    count = lax.axis_size("tp")
    if count != 4:
        return lax.psum_scatter(partial.astype(F32), "tp", scatter_dimension=1, tiled=True)
    me = lax.axis_index("tp")
    width = partial.shape[1] // 4

    def quarter(which):
        return lax.dynamic_slice_in_dim(partial, which * width, width, axis=1)

    to_core = jnp.concatenate([quarter(me ^ 1), quarter(me ^ 3)], axis=1)
    got = lax.ppermute(to_core, "tp", flip(4, 1)).astype(F32)
    to_chip = (quarter(me ^ 2).astype(F32) + got[:, width:]).astype(BF)
    from_chip = lax.ppermute(to_chip, "tp", flip(4, 2))
    return quarter(me).astype(F32) + got[:, :width] + from_chip.astype(F32)


def tensor_total(values):
    if lax.axis_size("tp") != 4:
        return lax.psum(values, "tp")
    values = values + lax.ppermute(values, "tp", flip(4, 1))
    return values + lax.ppermute(values, "tp", flip(4, 2))


def weight_gather(block, axis, chunks=1):
    count = lax.axis_size("fsdp")
    ctx = lax.axis_size("ctx")
    if count != 2 or ctx % 2:
        return lax.all_gather(block, "fsdp", axis=axis, tiled=True)
    me = lax.axis_index("fsdp")
    parity = lax.axis_index("ctx") % 2
    size = block.shape[axis]
    part = size // (2 * chunks)
    whole = jnp.concatenate([block, block], axis=axis)
    for c in range(chunks):
        mine = (2 * c + parity) * part
        other = (2 * c + 1 - parity) * part
        from_fsdp = lax.ppermute(
            lax.dynamic_slice_in_dim(block, mine, part, axis), "fsdp", flip(2, 1)
        )
        from_ctx = lax.ppermute(from_fsdp, "ctx", flip(ctx, 1))
        base = (1 - me) * size
        whole = lax.dynamic_update_slice_in_dim(whole, from_fsdp, base + mine, axis)
        whole = lax.dynamic_update_slice_in_dim(whole, from_ctx, base + other, axis)
    return whole


def ctx_total(term):
    ctx = lax.axis_size("ctx")
    if ctx != 4:
        return lax.psum(term, "ctx")
    place = lax.axis_index("ctx")
    ends = (place == 0) | (place == 3)
    pair = term + lax.ppermute(term, "ctx", [(0, 1), (3, 2)])
    whole = pair + lax.ppermute(pair, "ctx", [(1, 2), (2, 1)])
    back = lax.ppermute(whole, "ctx", [(1, 0), (2, 3)])
    return jnp.where(ends, back, whole)


def grad_total(left, right, axis, chunks=1):
    count = lax.axis_size("fsdp")
    if count != 2:
        term = mm_tn(left, right).astype(BF)
        term = lax.psum_scatter(term, "fsdp", scatter_dimension=axis, tiled=True)
        return ctx_total(term).astype(F32)
    me = lax.axis_index("fsdp")
    split = (left, right)[axis]
    size = split.shape[1] // 2
    part = size // chunks
    outs = []

    def product(start):
        piece = lax.dynamic_slice_in_dim(split, start, part, axis=1)
        return mm_tn(piece, right) if axis == 0 else mm_tn(left, piece)

    sent = []
    for c in range(chunks):
        away = product((1 - me) * size + c * part).astype(BF)
        sent.append(lax.ppermute(away, "fsdp", flip(2, 1)))
    for c in range(chunks):
        kept = product(me * size + c * part) + sent[c].astype(F32)
        outs.append(ctx_total(kept.astype(BF)).astype(F32))
    return jnp.concatenate(outs, axis=axis) if chunks > 1 else outs[0]


def vector_total(values):
    ctx = lax.axis_size("ctx")
    if lax.axis_size("fsdp") != 2 or ctx != 4:
        return lax.psum(values, ("fsdp", "ctx"))
    values = values + lax.ppermute(values, "fsdp", flip(2, 1))
    values = values + lax.ppermute(values, "ctx", flip(4, 1))
    return values + lax.ppermute(values, "ctx", flip(4, 3))


def earlier_blocks(rows):
    ctx = lax.axis_size("ctx")
    return [rows] + [
        lax.ppermute(rows, "ctx", [(i, i + k) for i in range(ctx - k)]) for k in range(1, ctx)
    ]


def sum_blocks(blocks):
    ctx = lax.axis_size("ctx")
    total = blocks[0]
    for k in range(1, ctx):
        got = lax.ppermute(
            blocks[k].astype(BF), "ctx", [(i, i - k) for i in range(k, ctx)]
        )
        total = total + got.astype(F32)
    return total


def on_device(
    tokens,
    segment_ids,
    positions,
    attn_gain,
    w_query,
    w_key,
    w_value,
    w_output,
    mlp_gain,
    w_gate,
    w_up,
    w_down,
    cotangent,
):
    seq_count, local_len, part_width = tokens.shape
    ctx = lax.axis_size("ctx")
    width = part_width * lax.axis_size("tp")
    full_len = local_len * ctx
    heads_here = w_query.shape[1] // HD
    kv_here = w_key.shape[1] // HD
    kv_width = kv_here * HD
    group_size = HQ // KV
    row_count = seq_count * local_len
    score_scale = HD ** (-0.5)
    place = lax.axis_index("ctx")
    me_tp = lax.axis_index("tp")

    token_rows = tokens.reshape(row_count, part_width)
    token_all = tensor_gather(token_rows)
    key_w = weight_gather(w_key, 0)
    value_w = weight_gather(w_value, 0)
    query_w = weight_gather(w_query, 0)
    output_w = weight_gather(w_output, 1)
    key_segs = jnp.concatenate(earlier_blocks(segment_ids), axis=1)
    gain_all = tensor_gather(attn_gain[None, :])
    gate_w = weight_gather(w_gate, 0, 2)
    up_w = weight_gather(w_up, 0, 2)
    down_w = weight_gather(w_down, 1, 2)

    cos_part, sin_part = angles(positions)
    key_places = jnp.concatenate(
        [(place - k) * local_len + jnp.arange(local_len, dtype=jnp.int32) for k in range(ctx)]
    )
    query_places = place * local_len + jnp.arange(local_len, dtype=jnp.int32)
    causal = query_places[:, None] >= key_places[None, :]

    token_f = token_all.astype(F32)
    scale_attn = lax.rsqrt(jnp.mean(token_f * token_f, axis=-1, keepdims=True) + EPS)
    normed = (token_f * scale_attn * gain_all).astype(BF)

    key_pre = mm(normed, key_w).reshape(seq_count, local_len, kv_here, HD)
    value_rows = mm(normed, value_w).astype(BF)
    key_rot = rotate(key_pre, cos_part, sin_part).astype(BF).reshape(row_count, kv_width)
    both = jnp.concatenate([key_rot, value_rows], axis=1).reshape(
        seq_count, local_len, 2 * kv_width
    )
    both_all = jnp.concatenate(earlier_blocks(both), axis=1)
    key_all, value_all = both_all[..., :kv_width], both_all[..., kv_width:]

    query_pre = mm(normed, query_w).reshape(seq_count, local_len, heads_here, HD)
    query_rot = rotate(query_pre, cos_part, sin_part).astype(BF)

    def masked_scores(query_seq, key_seq, seg_query, seg_key):
        grouped = query_seq.reshape(local_len, kv_here, group_size, HD)
        key_heads = key_seq.reshape(full_len, kv_here, HD)
        raw_scores = jnp.einsum(
            "qkgd,skd->kgqs", grouped, key_heads, preferred_element_type=F32
        )
        allowed = (seg_query[:, None] == seg_key[None, :]) & causal
        return (jnp.where(allowed, raw_scores * score_scale, NEG), grouped, key_heads)

    def attend_forward(pieces):
        query_seq, key_seq, value_seq, seg_query, seg_key = pieces
        scores, grouped, key_heads = masked_scores(query_seq, key_seq, seg_query, seg_key)
        row_max = jnp.max(scores, axis=-1, keepdims=True)
        exp_terms = jnp.exp(scores - row_max)
        row_total = jnp.sum(exp_terms, axis=-1, keepdims=True)
        attn_probs = (exp_terms / row_total).astype(BF)
        value_heads = value_seq.reshape(full_len, kv_here, HD)
        mixed_rows = jnp.einsum(
            "kgqs,skd->qkgd", attn_probs, value_heads, preferred_element_type=F32
        )
        log_total = (row_max + jnp.log(row_total))[..., 0]
        return (mixed_rows.astype(BF).reshape(local_len, heads_here * HD), log_total)

    attended, log_totals = lax.map(
        attend_forward, (query_rot, key_all, value_all, segment_ids, key_segs)
    )
    attended_flat = attended.reshape(row_count, heads_here * HD)
    branch = tensor_scatter(mm(attended_flat, output_w).astype(BF))
    resid_mid = token_rows.astype(F32) + branch

    gained = tensor_gather((resid_mid * mlp_gain).astype(BF))
    square_sum = tensor_total(jnp.sum(resid_mid * resid_mid, axis=-1))
    scale_mlp = lax.rsqrt(square_sum / width + EPS)[:, None]

    grad_all = tensor_gather(cotangent.reshape(row_count, part_width))
    gate_raw = mm(gained, gate_w)
    up_raw = mm(gained, up_w)
    gate_pre = gate_raw * scale_mlp
    up_pre = up_raw * scale_mlp
    gate_sig = jax.nn.sigmoid(gate_pre)
    gate_act = gate_pre * gate_sig
    activated = (gate_act * up_pre).astype(BF)
    down_grad = grad_total(activated, grad_all, 1, 2)

    act_grad = mm_nt(grad_all, down_w)
    gate_grad = (
        scale_mlp * act_grad * up_pre * gate_sig * (1.0 + gate_pre * (1.0 - gate_sig))
    ).astype(BF)
    up_grad = (scale_mlp * act_grad * gate_act).astype(BF)
    gate_w_grad = grad_total(gained, gate_grad, 0, 2)
    up_w_grad = grad_total(gained, up_grad, 0, 2)
    mid_inner = tensor_total(
        jnp.sum(gate_grad.astype(F32) * gate_raw + up_grad.astype(F32) * up_raw, axis=-1)
    )[:, None]
    scaled_grad = tensor_scatter((mm_nt(gate_grad, gate_w) + mm_nt(up_grad, up_w)).astype(BF))

    mlp_out = tensor_scatter(mm(activated, down_w).astype(BF))
    output = (resid_mid + mlp_out).astype(BF)

    mlp_gain_part = jnp.sum(scaled_grad * resid_mid, axis=0)
    resid_mid_grad = (
        cotangent.reshape(row_count, part_width).astype(F32)
        + mlp_gain * scaled_grad
        - resid_mid * (scale_mlp * scale_mlp * mid_inner / width)
    )
    branch_grad = tensor_gather(resid_mid_grad.astype(BF))
    attended_grad = mm_nt(branch_grad, output_w).astype(BF)
    attended_grad = attended_grad.reshape(seq_count, local_len, heads_here * HD)
    output_w_grad = grad_total(attended_flat, branch_grad, 1)

    def attend_backward(pieces):
        query_seq, key_seq, value_seq, seg_query, seg_key, log_total, mixed_grad = pieces
        scores, grouped, key_heads = masked_scores(query_seq, key_seq, seg_query, seg_key)
        attn_probs = jnp.exp(scores - log_total[..., None])
        probs_low = attn_probs.astype(BF)
        value_heads = value_seq.reshape(full_len, kv_here, HD)
        grad_heads = mixed_grad.reshape(local_len, kv_here, group_size, HD)
        prob_grad = jnp.einsum(
            "qkgd,skd->kgqs", grad_heads, value_heads, preferred_element_type=F32
        )
        inner_sum = jnp.sum(attn_probs * prob_grad, axis=-1, keepdims=True)
        score_grad = (score_scale * attn_probs * (prob_grad - inner_sum)).astype(BF)
        query_grad = jnp.einsum(
            "kgqs,skd->qkgd", score_grad, key_heads, preferred_element_type=F32
        )
        key_grad = jnp.einsum(
            "kgqs,qkgd->skd", score_grad, grouped, preferred_element_type=F32
        )
        value_grad = jnp.einsum(
            "kgqs,qkgd->skd", probs_low, grad_heads, preferred_element_type=F32
        )
        return (
            query_grad.reshape(local_len, heads_here, HD),
            key_grad.reshape(full_len, kv_width),
            value_grad.reshape(full_len, kv_width),
        )

    query_grads, key_grads, value_grads = lax.map(
        attend_backward,
        (query_rot, key_all, value_all, segment_ids, key_segs, log_totals, attended_grad),
    )
    both_grads = jnp.concatenate([key_grads, value_grads], axis=2)
    both_sum = sum_blocks(
        [both_grads[:, k * local_len : (k + 1) * local_len] for k in range(ctx)]
    )
    key_sum, value_sum = both_sum[..., :kv_width], both_sum[..., kv_width:]
    query_grad_pre = unrotate(query_grads, cos_part, sin_part).astype(BF).reshape(row_count, -1)
    key_grad_pre = unrotate(
        key_sum.reshape(seq_count, local_len, kv_here, HD), cos_part, sin_part
    )
    key_grad_pre = key_grad_pre.astype(BF).reshape(row_count, -1)
    value_grad_pre = value_sum.astype(BF).reshape(row_count, -1)

    query_w_grad = grad_total(normed, query_grad_pre, 0)
    key_w_grad = grad_total(normed, key_grad_pre, 0)
    value_w_grad = grad_total(normed, value_grad_pre, 0)

    in_inner = jnp.sum(query_grads * query_rot.astype(F32), axis=(2, 3)).reshape(row_count)
    in_inner = in_inner + jnp.sum(both_sum * both.astype(F32), axis=2).reshape(row_count)
    in_inner = tensor_total(in_inner)[:, None]
    normed_grad = mm_nt(query_grad_pre, query_w) + mm_nt(key_grad_pre, key_w)
    normed_grad = tensor_scatter((normed_grad + mm_nt(value_grad_pre, value_w)).astype(BF))

    own_tokens = token_rows.astype(F32)
    attn_gain_part = jnp.sum(normed_grad * own_tokens * scale_attn, axis=0)
    input_grad = (
        resid_mid_grad
        + scale_attn * attn_gain * normed_grad
        - own_tokens * (scale_attn * scale_attn * in_inner / width)
    )
    attn_gain_grad = vector_total(attn_gain_part)
    mlp_gain_grad = vector_total(mlp_gain_part)
    shape = (seq_count, local_len, part_width)
    return (
        output.reshape(shape),
        input_grad.reshape(shape),
        attn_gain_grad,
        query_w_grad,
        key_w_grad,
        value_w_grad,
        output_w_grad,
        mlp_gain_grad,
        gate_w_grad,
        up_w_grad,
        down_grad,
    )


def solution(mesh):
    rows = P("fsdp", "ctx", "tp")
    placed = (
        rows,
        P("fsdp", "ctx"),
        P("fsdp", "ctx"),
        P("tp"),
        P("fsdp", "tp"),
        P("fsdp", "tp"),
        P("fsdp", "tp"),
        P("tp", "fsdp"),
        P("tp"),
        P("fsdp", "tp"),
        P("fsdp", "tp"),
        P("tp", "fsdp"),
        rows,
    )
    return jax.shard_map(
        on_device,
        mesh=mesh,
        in_specs=placed,
        out_specs=(
            rows,
            rows,
            P("tp"),
            P("fsdp", "tp"),
            P("fsdp", "tp"),
            P("fsdp", "tp"),
            P("tp", "fsdp"),
            P("tp"),
            P("fsdp", "tp"),
            P("fsdp", "tp"),
            P("tp", "fsdp"),
        ),
        check_vma=False,
    )
```

```python
import functools
import math

import jax
import jax.numpy as jnp
from jax import lax
from jax.experimental import pallas as pl
from jax.experimental.pallas import tpu as pltpu
from jax.sharding import PartitionSpec as P

HQ = 32
KV = 8
HD = 64

THETA = 500000.0
EPS = 1e-05
NEG = -1e30
BF = jnp.bfloat16
F32 = jnp.float32
SPLITS = 4
ANY = pl.BlockSpec(memory_space=pl.ANY)


def nn(left, right):
    return jnp.dot(left, right, preferred_element_type=F32)


def tn(left, right):
    return lax.dot_general(left, right, (((0,), (0,)), ((), ())), preferred_element_type=F32)


def nt(left, right):
    return lax.dot_general(left, right, (((1,), (1,)), ((), ())), preferred_element_type=F32)


def nothing(*refs):
    pass


def after(value, *others):
    return pl.pallas_call(
        nothing,
        out_shape=jax.ShapeDtypeStruct(value.shape, value.dtype),
        in_specs=[ANY] * (1 + len(others)),
        out_specs=ANY,
        input_output_aliases={0: 0},
        name="after",
    )(value, *others)


def turn(rows, cos, sin):
    width = rows.shape[1]
    lane = lax.broadcasted_iota(jnp.int32, rows.shape, 1)
    other = jnp.where(
        lane % HD < HD // 2,
        pltpu.roll(rows, width - HD // 2, 1),
        pltpu.roll(rows, HD // 2, 1),
    )
    reps = width // 128
    return rows * jnp.concatenate([cos] * reps, axis=1) + other * jnp.concatenate(
        [sin] * reps, axis=1
    )


def heads_down(rows, first, count):
    return jnp.concatenate(
        [rows[:, (first + g) * HD : (first + g + 1) * HD] for g in range(count)], axis=0
    )


def block_mask(k, seq, seqs, segq_ref, segk_ref, rows, group):
    at = k * seqs + seq
    same = segk_ref[:, at : at + 1] == segq_ref[seq : seq + 1, :]
    if k == 0:
        key_at = lax.broadcasted_iota(jnp.int32, (rows, rows), 0)
        query_at = lax.broadcasted_iota(jnp.int32, (rows, rows), 1)
        same = same & (key_at <= query_at)
    return jnp.concatenate([same] * group, axis=1)


def attend_fwd_kernel(seq, seqs, kv_heads, group, blocks, flags, q_ref, *refs):
    kv_refs = refs[:blocks]
    segq_ref, segk_ref, o_ref, lse_ref, m_s, l_s, acc_s = refs[blocks:]
    rows = q_ref.shape[0]
    for h in range(kv_heads):
        qg = heads_down(q_ref[...], h * group, group) * jnp.asarray(HD**-0.5, BF)
        for k in range(blocks):

            def step(k=k):
                key = kv_refs[k][0, :, h * HD : (h + 1) * HD]
                val = kv_refs[k][0, :, (kv_heads + h) * HD : (kv_heads + h + 1) * HD]
                mask = block_mask(k, seq, seqs, segq_ref, segk_ref, rows, group)
                scores = jnp.where(mask, nt(key, qg), NEG)
                top = jnp.max(scores, axis=0, keepdims=True)
                if k == 0:
                    probs = jnp.exp(scores - top)
                    m_s[...] = top
                    l_s[...] = jnp.sum(probs, axis=0, keepdims=True)
                    acc_s[...] = tn(val, probs.astype(BF))
                else:
                    new = jnp.maximum(m_s[...], top)
                    fix = jnp.exp(m_s[...] - new)
                    probs = jnp.exp(scores - new)
                    m_s[...] = new
                    l_s[...] = l_s[...] * fix + jnp.sum(probs, axis=0, keepdims=True)
                    acc_s[...] = acc_s[...] * fix + tn(val, probs.astype(BF))

            if k == 0:
                step()
            else:
                pl.when(flags[seq, k] != 0)(step)
        out = (acc_s[...] / l_s[...]).T.astype(BF)
        for g in range(group):
            o_ref[:, (h * group + g) * HD : (h * group + g + 1) * HD] = out[
                g * rows : (g + 1) * rows
            ]
        lse_ref[0, h : h + 1, :] = m_s[...] + jnp.log(l_s[...])


def attend_bwd_kernel(seq, seqs, kv_heads, group, blocks, flags, *refs):
    q_ref, do_ref, o_ref, lse_ref, cos_ref, sin_ref = refs[:6]
    kv_refs = refs[6 : 6 + blocks]
    segq_ref, segk_ref, dq_ref, j_ref = refs[6 + blocks : 10 + blocks]
    dkv_refs = refs[10 + blocks : 10 + 2 * blocks]
    dq_s = refs[10 + 2 * blocks]
    rows = q_ref.shape[0]
    ones = jnp.ones((8, HD), BF)
    for h in range(kv_heads):
        qg = heads_down(q_ref[...], h * group, group) * jnp.asarray(HD**-0.5, BF)
        dog = heads_down(do_ref[...], h * group, group)
        og = heads_down(o_ref[...], h * group, group)
        prod = dog.astype(F32) * og.astype(F32)
        high = prod.astype(BF)
        low = (prod - high.astype(F32)).astype(BF)
        delta = (nt(ones, high) + nt(ones, low))[0:1]
        lse = lse_ref[0, h : h + 1, :]
        key_at = slice(h * HD, (h + 1) * HD)
        val_at = slice((kv_heads + h) * HD, (kv_heads + h + 1) * HD)
        for k in range(blocks):

            def step(k=k):
                key = kv_refs[k][0, :, key_at]
                val = kv_refs[k][0, :, val_at]
                mask = block_mask(k, seq, seqs, segq_ref, segk_ref, rows, group)
                probs = jnp.exp(jnp.where(mask, nt(key, qg), NEG) - lse)
                score_grad = (probs * (nt(val, dog) - delta)).astype(BF)
                kind = dkv_refs[k].dtype
                dkv_refs[k][0, :, key_at] = nn(score_grad, qg).astype(kind)
                dkv_refs[k][0, :, val_at] = nn(probs.astype(BF), dog).astype(kind)
                dq = tn(key, score_grad)
                dq_s[h] = dq if k == 0 else dq_s[h] + dq

            if k == 0:
                step()
            else:
                pl.when(flags[seq, k] != 0)(step)

                @pl.when(flags[seq, k] == 0)
                def _(k=k):
                    zero = jnp.zeros((rows, HD), dkv_refs[k].dtype)
                    dkv_refs[k][0, :, key_at] = zero
                    dkv_refs[k][0, :, val_at] = zero

    turned = [(dq_s[h] * (HD**-0.5)).T for h in range(kv_heads)]
    dq = jnp.concatenate(
        [t[g * rows : (g + 1) * rows] for t in turned for g in range(group)], axis=1
    )
    inner = dq * q_ref[...].astype(F32)
    total = inner[:, :128]
    for i in range(1, dq.shape[1] // 128):
        total = total + inner[:, i * 128 : (i + 1) * 128]
    j_ref[...] = total
    dq_ref[...] = turn(dq, cos_ref[...], -sin_ref[...]).astype(BF)


def attend_call(kernel, seq, q, rows_in, whole_in, kvs, segq, segk, flags, outs, scratch, work, name):
    seqs, rows = segq.shape
    kv_heads = kvs[0].shape[2] // (2 * HD)
    group = q.shape[1] // (HD * kv_heads)
    blocks = len(kvs)

    def whole(shape):
        return pl.BlockSpec(shape, lambda i, *_: (0,) * len(shape))

    def of_seq(array):
        return pl.BlockSpec((rows, array.shape[1]), lambda i, *_: (seq, 0))

    kv_spec = pl.BlockSpec((1, rows, kvs[0].shape[2]), lambda i, *_: (seq, 0, 0))
    return pl.pallas_call(
        functools.partial(kernel, seq, seqs, kv_heads, group, blocks),
        grid_spec=pltpu.PrefetchScalarGridSpec(
            num_scalar_prefetch=1,
            grid=(1,),
            in_specs=[of_seq(q)]
            + [of_seq(a) for a in rows_in[:1]]
            + [whole(a.shape) for a in whole_in]
            + [of_seq(a) for a in rows_in[1:]]
            + [kv_spec] * blocks
            + [whole(segq.shape), whole(segk.shape)],
            out_specs=[whole(shape) for shape, _ in outs],
            scratch_shapes=[pltpu.VMEM(shape, F32) for shape in scratch],
        ),
        out_shape=[jax.ShapeDtypeStruct(shape, kind) for shape, kind in outs],
        compiler_params=pltpu.CompilerParams(vmem_limit_bytes=40 * 2**20),
        cost_estimate=pl.CostEstimate(flops=work, bytes_accessed=10**7, transcendentals=10**6),
        name=name,
    )(flags, q, *rows_in[:1], *whole_in, *rows_in[1:], *kvs, segq, segk)


def attend_forward(seq, q, kvs, segq, segk, flags):
    rows = segq.shape[1]
    kv_heads = kvs[0].shape[2] // (2 * HD)
    long = q.shape[1] // (HD * kv_heads) * rows
    return attend_call(
        attend_fwd_kernel, seq, q, [], [], kvs, segq, segk, flags,
        [((rows, q.shape[1]), BF), ((1, kv_heads, long), F32)],
        [(1, long), (1, long), (HD, long)], 10**9, "attend_forward",
    )


def attend_backward(seq, q, do, o, lse, cos, sin, kvs, segq, segk, flags):
    rows = segq.shape[1]
    kv_width = kvs[0].shape[2]
    kv_heads = kv_width // (2 * HD)
    long = q.shape[1] // (HD * kv_heads) * rows
    grads = [((1, rows, kv_width), F32 if k == 0 else BF) for k in range(len(kvs))]
    return attend_call(
        attend_bwd_kernel, seq, q, [do, cos, sin], [o, lse], kvs, segq, segk, flags,
        [((rows, q.shape[1]), BF), ((rows, 128), F32)] + grads,
        [(kv_heads, HD, long)], 2 * 10**9, "attend_backward",
    )


def turn_kernel(turned, pre_ref, cos_ref, sin_ref, out_ref):
    pre = pre_ref[...]
    out_ref[:, :turned] = turn(pre[:, :turned], cos_ref[...], sin_ref[...]).astype(BF)
    if turned < pre.shape[1]:
        out_ref[:, turned:] = pre[:, turned:].astype(BF)


def turn_rows(pre, cos, sin, turned):
    return pl.pallas_call(
        functools.partial(turn_kernel, turned),
        out_shape=jax.ShapeDtypeStruct(pre.shape, BF),
        compiler_params=pltpu.CompilerParams(vmem_limit_bytes=32 * 2**20),
        name="turn_rows",
    )(pre, cos, sin)


def flip(count, bit):
    return [(i, i ^ bit) for i in range(count)]


class Plan:
    def __init__(self):
        self.fsdp = lax.axis_size("fsdp")
        self.ctx = lax.axis_size("ctx")
        self.tp = lax.axis_size("tp")
        self.y = lax.axis_index("fsdp")
        self.z = lax.axis_index("ctx")
        self.t = lax.axis_index("tp")
        self.pairs = self.fsdp == 2 and self.ctx == 4 and self.tp == 4
        self.parity = self.z % 2
        if self.pairs:
            base = 2 * (1 - self.y)
            self.order = [2 * self.y, 2 * self.y + 1, base + self.parity, base + 1 - self.parity]

    def slot(self, quarter):
        if not self.pairs:
            return quarter
        low = quarter % 2
        return jnp.where(quarter // 2 == self.y, low, 2 + (low ^ self.parity))

    def own(self, wide):
        return wide[:, : wide.shape[1] // 2]

    def away(self, wide):
        quarter = wide.shape[1] // 4
        return jnp.concatenate(
            [
                lax.dynamic_slice_in_dim(wide, (2 + (r ^ self.parity)) * quarter, quarter, axis=1)
                for r in range(2)
            ],
            axis=1,
        )


class TensorGather:
    def __init__(self, plan, part):
        self.plan = plan
        if plan.tp != 4:
            self.out = lax.all_gather(part, "tp", axis=1, tiled=True)
            return
        self.out = None
        self.part = part
        self.far = lax.ppermute(part, "tp", flip(4, 2))
        self.near = lax.ppermute(part, "tp", flip(4, 1))

    def relay(self):
        if self.out is None:
            self.far_near = lax.ppermute(self.far, "tp", flip(4, 1))

    def pieces(self):
        plan = self.plan
        order = plan.order if plan.pairs else list(range(4))
        held = [self.part, self.near, self.far, self.far_near]
        pieces = []
        for quarter in order:
            which = quarter ^ plan.t
            low = jnp.where(which % 2 == 1, held[1], held[0])
            high = jnp.where(which % 2 == 1, held[3], held[2])
            pieces.append(jnp.where(which >= 2, high, low))
        return pieces

    def whole(self):
        return jnp.concatenate(self.pieces(), axis=1) if self.out is None else self.out


class TensorScatter:
    def __init__(self, plan, terms):
        self.plan = plan
        self.terms = terms
        if plan.tp != 4:
            self.out = lax.psum_scatter(terms.astype(F32), "tp", scatter_dimension=1, tiled=True)
            return
        self.out = None
        self.width = terms.shape[1] // 4
        near = jnp.concatenate([self.quarter(plan.t ^ 1), self.quarter(plan.t ^ 3)], axis=1)
        self.got = lax.ppermute(near, "tp", flip(4, 1))

    def quarter(self, which):
        start = self.plan.slot(which) * self.width
        return lax.dynamic_slice_in_dim(self.terms, start, self.width, axis=1)

    def cross(self):
        if self.out is None:
            got = self.got[:, self.width :].astype(F32)
            far = (self.quarter(self.plan.t ^ 2).astype(F32) + got).astype(BF)
            self.far = lax.ppermute(far, "tp", flip(4, 2))

    def total(self):
        if self.out is not None:
            return self.out
        own = self.quarter(self.plan.t).astype(F32) + self.got[:, : self.width].astype(F32)
        return own + self.far.astype(F32)


def tensor_total(plan, values):
    if plan.tp != 4:
        return lax.psum(values, "tp")
    values = values + lax.ppermute(values, "tp", flip(4, 1))
    return values + lax.ppermute(values, "tp", flip(4, 2))


class Weight:
    def __init__(self, plan, block, axis, *behind):
        self.plan, self.block, self.axis = plan, block, axis
        if not plan.pairs:
            whole = lax.all_gather(block, "fsdp", axis=axis, tiled=True)
            self.out = whole
            return
        self.out = None
        part = block.shape[axis] // 2
        sent = lax.dynamic_slice_in_dim(block, plan.parity * part, part, axis)
        if behind:
            sent = after(sent, *behind)
        self.got = lax.ppermute(sent, "fsdp", flip(2, 1))

    def relay(self, *behind):
        if self.out is None:
            sent = after(self.got, *behind) if behind else self.got
            self.got = sent
            self.got_ctx = lax.ppermute(sent, "ctx", flip(4, 1))

    def whole(self):
        if self.out is not None:
            return self.out
        return jnp.concatenate([self.block, self.got, self.got_ctx], axis=self.axis)


class Grad:
    def __init__(self, plan, left, right, axis):
        self.plan, self.left, self.right, self.axis = plan, left, right, axis
        if plan.pairs:
            away = tn(left[0], right) if axis == 0 else tn(left, right[0])
            self.sent = lax.ppermute(away.astype(BF), "fsdp", flip(2, 1))
        else:
            terms = tn(left, right).astype(BF)
            self.term = lax.psum_scatter(terms, "fsdp", scatter_dimension=axis, tiled=True)

    def merge(self, *behind):
        plan = self.plan
        if plan.pairs:
            got = after(self.sent, *behind) if behind else self.sent
            left, right = self.left, self.right
            own = tn(left[1], right) if self.axis == 0 else tn(left, right[1])
            self.term = (own + got.astype(F32)).astype(BF)
        if plan.ctx == 4:
            self.pair = lax.ppermute(self.term, "ctx", [(0, 1), (3, 2)])
        else:
            self.term = lax.psum(self.term, "ctx")
        return self.term

    def middle(self, *behind):
        if self.plan.ctx == 4:
            got = after(self.pair, *behind) if behind else self.pair
            self.term = self.term + got
            self.pair = lax.ppermute(self.term, "ctx", [(1, 2), (2, 1)])
        return self.term

    def back(self, *behind):
        if self.plan.ctx == 4:
            got = after(self.pair, *behind) if behind else self.pair
            self.term = self.term + got
            self.pair = lax.ppermute(self.term, "ctx", [(1, 0), (2, 3)])
        return self.term

    def total(self, *behind):
        if self.plan.ctx == 4:
            got = after(self.pair, *behind) if behind else self.pair
            ends = (self.plan.z == 0) | (self.plan.z == 3)
            self.term = jnp.where(ends, got, self.term)
        return self.term.astype(F32)


def vector_total(plan, values):
    if not plan.pairs:
        return lax.psum(values, ("fsdp", "ctx"))
    values = values + lax.ppermute(values, "fsdp", flip(2, 1))
    values = values + lax.ppermute(values, "ctx", flip(4, 1))
    return values + lax.ppermute(values, "ctx", flip(4, 3))


def earlier_blocks(plan, rows):
    return [rows] + [
        lax.ppermute(rows, "ctx", [(i, i + k) for i in range(plan.ctx - k)])
        for k in range(1, plan.ctx)
    ]


def on_device(
    tokens,
    segment_ids,
    positions,
    attn_gain,
    w_query,
    w_key,
    w_value,
    w_output,
    mlp_gain,
    w_gate,
    w_up,
    w_down,
    cotangent,
):
    plan = Plan()
    seqs, length, part_width = tokens.shape
    rows = seqs * length
    width = part_width * plan.tp
    kv_width = w_key.shape[1]
    hidden = w_gate.shape[1]
    span = hidden // SPLITS
    ranges = [slice(j * span, (j + 1) * span) for j in range(SPLITS)]
    token_rows = tokens.reshape(rows, part_width)
    cot_rows = cotangent.reshape(rows, part_width)

    token_part = TensorGather(plan, token_rows)
    kv_weight = Weight(plan, jnp.concatenate([w_key, w_value], axis=1), 0)
    segk = jnp.concatenate(earlier_blocks(plan, segment_ids), axis=0)
    gains = TensorGather(plan, jnp.stack([attn_gain]))
    q_weight = Weight(plan, w_query, 0)
    o_weight = Weight(plan, w_output, 1)
    queue = [kv_weight, q_weight, o_weight]

    def behind_queue():
        return [queue[-3].got] if plan.pairs else []

    gu_weights, down_weights = [], []
    for at in ranges:
        block = jnp.concatenate([w_gate[:, at], w_up[:, at]], axis=1)
        gu_weights.append(Weight(plan, block, 0, *behind_queue()))
        queue.append(gu_weights[-1])
    for at in ranges:
        down_weights.append(Weight(plan, w_down[at], 1, *behind_queue()))
        queue.append(down_weights[-1])

    frequency = jnp.exp(jnp.arange(HD // 2, dtype=F32) * (-2.0 * math.log(THETA) / HD))
    turn_angle = positions.reshape(rows, 1).astype(F32) * frequency
    cos_half, sin_half = jnp.cos(turn_angle), jnp.sin(turn_angle)
    cos = jnp.concatenate([cos_half] * 4, axis=1)
    sin = jnp.concatenate([-sin_half, sin_half] * 2, axis=1)
    first_seg = segment_ids[:, 0]
    flags = jnp.stack(
        [(segk[k * seqs : (k + 1) * seqs, -1] == first_seg) for k in range(plan.ctx)], axis=1
    ).astype(jnp.int32)
    segk = segk.T

    kv_weight.relay()
    token_part.relay()
    gains.relay()
    token_all = token_part.whole().astype(F32)
    scale_attn = lax.rsqrt(jnp.mean(token_all * token_all, axis=-1, keepdims=True) + EPS)
    normed = (token_all * scale_attn * gains.whole()).astype(BF)
    q_weight.relay()
    o_weight.relay()
    kv_w = kv_weight.whole()
    kv_own = turn_rows(nn(normed, kv_w), cos, sin, kv_width)
    kv_blocks = earlier_blocks(plan, kv_own.reshape(seqs, length, 2 * kv_width))
    q_w = q_weight.whole()
    query_rot = turn_rows(nn(normed, q_w), cos, sin, w_query.shape[1])
    cot_part = TensorGather(plan, after(cot_rows, token_part.far))
    cot_part.relay()
    o_w = o_weight.whole()

    scatters, attended, log_totals = [], [], []
    for s in range(seqs):
        out, log_total = attend_forward(s, query_rot, kv_blocks, segment_ids, segk, flags)
        attended.append(out)
        log_totals.append(log_total)
        scatters.append(TensorScatter(plan, nn(out, o_w).astype(BF)))
    for w in gu_weights:
        w.relay()
    resid_parts, gained_parts = [], []
    for s in range(seqs):
        scatters[s].cross()
        resid = token_rows[s * length : (s + 1) * length].astype(F32) + scatters[s].total()
        resid_parts.append(resid)
        gained_parts.append(TensorGather(plan, (resid * mlp_gain).astype(BF)))
    resid_mid = jnp.concatenate(resid_parts, axis=0)
    square_sum = tensor_total(plan, jnp.sum(resid_mid * resid_mid, axis=-1))
    scale_mlp = lax.rsqrt(square_sum / width + EPS)[:, None]
    for part in gained_parts:
        part.relay()
    gained = jnp.concatenate([part.whole() for part in gained_parts], axis=0)
    cot_all = cot_part.whole()

    if plan.pairs:
        gained_sides = (plan.away(gained), plan.own(gained))
        cot_sides = (plan.away(cot_all), plan.own(cot_all))
    raws, acts, grads_down = [], [], []
    for j in range(SPLITS):
        raw = nn(gained, gu_weights[j].whole())
        raws.append(raw)
        gate_pre, up_pre = raw[:, :span] * scale_mlp, raw[:, span:] * scale_mlp
        activated = (gate_pre * jax.nn.sigmoid(gate_pre) * up_pre).astype(BF)
        acts.append(activated)
        grads_down.append(Grad(plan, activated, cot_sides if plan.pairs else cot_all, 1))
    for w in down_weights:
        w.relay()
    down_ws = [w.whole() for w in down_weights]
    gu_grads, grads_gu, mid_inner = [], [], 0.0
    half = part_width
    for j in range(SPLITS):
        raw = raws[j]
        gate_pre, up_pre = raw[:, :span] * scale_mlp, raw[:, span:] * scale_mlp
        gate_sig = jax.nn.sigmoid(gate_pre)
        act_grad = nt(cot_all, down_ws[j]) * scale_mlp
        gate_grad = act_grad * up_pre * gate_sig * (1.0 + gate_pre * (1.0 - gate_sig))
        up_grad = act_grad * gate_pre * gate_sig
        gu_grad = jnp.concatenate([gate_grad, up_grad], axis=1).astype(BF)
        mid_inner = mid_inner + jnp.sum(gu_grad.astype(F32) * raw, axis=-1)
        gu_grads.append(gu_grad)
        if plan.pairs:
            for r in range(2):
                at = slice(r * half, (r + 1) * half)
                sides = (gained_sides[0][:, at], gained_sides[1][:, at])
                grads_gu.append(Grad(plan, sides, gu_grad, 0))
        else:
            grads_gu.append(Grad(plan, gained, gu_grad, 0))
    mid_inner = tensor_total(plan, mid_inner)[:, None]
    gu_all = jnp.concatenate([w.whole() for w in gu_weights], axis=1)
    mid_scatter = TensorScatter(plan, nt(jnp.concatenate(gu_grads, axis=1), gu_all).astype(BF))
    for g in grads_down:
        g.merge()
    mid_scatter.cross()
    out_scatter = TensorScatter(
        plan, nn(jnp.concatenate(acts, axis=1), jnp.concatenate(down_ws, axis=0)).astype(BF)
    )
    out_scatter.cross()
    scaled_grad = mid_scatter.total()
    mlp_gain_part = jnp.sum(scaled_grad * resid_mid, axis=0)
    resid_mid_grad = (
        cot_rows.astype(F32)
        + mlp_gain * scaled_grad
        - resid_mid * (scale_mlp * scale_mlp * mid_inner / width)
    )
    branch_part = TensorGather(plan, resid_mid_grad.astype(BF))
    output = (resid_mid + out_scatter.total()).astype(BF)
    branch_part.relay()
    branch_grad = branch_part.whole()

    attended_grad = nt(branch_grad, o_w).astype(BF)
    attended_all = jnp.concatenate(attended, axis=0)
    bg_sides = (plan.away(branch_grad), plan.own(branch_grad)) if plan.pairs else branch_grad
    grad_o = Grad(plan, attended_all, bg_sides, 1)
    results = [
        attend_backward(
            s, query_rot, attended_grad, attended[s], log_totals[s], cos, sin, kv_blocks,
            segment_ids, segk, flags,
        )
        for s in range(seqs)
    ]
    query_grad = jnp.concatenate([r[0] for r in results], axis=0)
    in_inner = jnp.sum(jnp.concatenate([r[1] for r in results], axis=0), axis=1)
    kv_terms = [jnp.concatenate([r[2 + k] for r in results], axis=0) for k in range(plan.ctx)]
    kv_sum = kv_terms[0]
    for k in range(1, plan.ctx):
        got = lax.ppermute(kv_terms[k], "ctx", [(i, i - k) for i in range(k, plan.ctx)])
        kv_sum = kv_sum + got.astype(F32)
    kv_sum = kv_sum.reshape(rows, 2 * kv_width)
    kv_grad = turn_rows(kv_sum, cos, -sin, kv_width)
    in_inner = in_inner + jnp.sum(kv_sum * kv_own.astype(F32), axis=1)
    in_inner = tensor_total(plan, in_inner)[:, None]
    normed_sides = (plan.away(normed), plan.own(normed)) if plan.pairs else normed
    in_terms = nt(query_grad, q_w) + nt(kv_grad, kv_w)
    in_scatter = TensorScatter(plan, in_terms.astype(BF))
    grad_kv = Grad(plan, normed_sides, kv_grad, 0)
    grad_q = Grad(plan, normed_sides, query_grad, 0)
    in_scatter.cross()
    normed_grad = in_scatter.total()
    own_tokens = token_rows.astype(F32)
    attn_gain_part = jnp.sum(normed_grad * own_tokens * scale_attn, axis=0)
    input_grad = (
        resid_mid_grad
        + scale_attn * attn_gain * normed_grad
        - own_tokens * (scale_attn * scale_attn * in_inner / width)
    )
    gain_grads = vector_total(plan, jnp.concatenate([attn_gain_part, mlp_gain_part]))

    chain = grads_down + grads_gu + [grad_o, grad_kv, grad_q]
    last = []
    steps = len(chain) + 3
    outs = [None] * len(chain)
    for i in range(steps):
        mark = []
        if i < len(chain):
            if chain[i] in grads_down:
                mark.append(chain[i].term) if hasattr(chain[i], "term") else None
            else:
                mark.append(chain[i].merge(*last))
        if 0 <= i - 1 < len(chain):
            mark.append(chain[i - 1].middle(*last))
        if 0 <= i - 2 < len(chain):
            mark.append(chain[i - 2].back(*last))
        if 0 <= i - 3 < len(chain):
            outs[i - 3] = chain[i - 3].total(*last)
        last = [m for m in mark if m is not None]
    n = len(grads_down)
    m = n + len(grads_gu)
    down_grad = jnp.concatenate(outs[:n], axis=0)
    per = len(grads_gu) // SPLITS
    gu = [jnp.concatenate(outs[n + j * per : n + (j + 1) * per], axis=0) for j in range(SPLITS)]
    gate_w_grad = jnp.concatenate([g[:, :span] for g in gu], axis=1)
    up_w_grad = jnp.concatenate([g[:, span:] for g in gu], axis=1)
    output_w_grad, kv_w_grad, query_w_grad = outs[m:]
    shape = (seqs, length, part_width)
    return (
        output.reshape(shape),
        input_grad.reshape(shape),
        gain_grads[:part_width],
        query_w_grad,
        kv_w_grad[:, :kv_width],
        kv_w_grad[:, kv_width:],
        output_w_grad,
        gain_grads[part_width:],
        gate_w_grad,
        up_w_grad,
        down_grad,
    )


def solution(mesh):
    rows = P("fsdp", "ctx", "tp")
    per_token = P("fsdp", "ctx")
    columns = P("fsdp", "tp")
    across = P("tp", "fsdp")
    gain = P("tp")
    return jax.shard_map(
        on_device,
        mesh=mesh,
        in_specs=(
            rows, per_token, per_token, gain, columns, columns, columns, across, gain,
            columns, columns, across, rows,
        ),
        out_specs=(
            rows, rows, gain, columns, columns, columns, across, gain, columns, columns, across,
        ),
        check_vma=False,
    )
```

```python
import functools
import math

import jax
import jax.numpy as jnp
from jax import lax
from jax.experimental import pallas as pl
from jax.experimental.pallas import tpu as pltpu
from jax.sharding import PartitionSpec as P

HQ = 32
KV = 8
HD = 64

THETA = 500000.0
EPS = 1e-05
NEG = -1e30
BF = jnp.bfloat16
F32 = jnp.float32
SPLITS = 4
ANY = pl.BlockSpec(memory_space=pl.ANY)


def nn(left, right):
    return jnp.dot(left, right, preferred_element_type=F32)


def tn(left, right):
    return lax.dot_general(left, right, (((0,), (0,)), ((), ())), preferred_element_type=F32)


def nt(left, right):
    return lax.dot_general(left, right, (((1,), (1,)), ((), ())), preferred_element_type=F32)


def nothing(*refs):
    pass


def after(value, *others):
    return pl.pallas_call(
        nothing,
        out_shape=jax.ShapeDtypeStruct(value.shape, value.dtype),
        in_specs=[ANY] * (1 + len(others)),
        out_specs=ANY,
        input_output_aliases={0: 0},
        name="after",
    )(value, *others)


def turn(rows, cos, sin):
    width = rows.shape[1]
    lane = lax.broadcasted_iota(jnp.int32, rows.shape, 1)
    other = jnp.where(
        lane % HD < HD // 2,
        pltpu.roll(rows, width - HD // 2, 1),
        pltpu.roll(rows, HD // 2, 1),
    )
    reps = width // 128
    return rows * jnp.concatenate([cos] * reps, axis=1) + other * jnp.concatenate(
        [sin] * reps, axis=1
    )


def heads_down(rows, first, count):
    return jnp.concatenate(
        [rows[:, (first + g) * HD : (first + g + 1) * HD] for g in range(count)], axis=0
    )


ID_ROWS = 16


def block_ids(kv_ref, rows):
    return kv_ref[0, rows : rows + ID_ROWS, :rows].astype(F32)[0:1]


def block_mask(k, segq_ref, kv_ref, rows, group):
    ids = jnp.broadcast_to(block_ids(kv_ref, rows), (8, rows))
    same = ids.T[:, 0:1] == segq_ref[0]
    if k == 0:
        key_at = lax.broadcasted_iota(jnp.int32, (rows, rows), 0)
        query_at = lax.broadcasted_iota(jnp.int32, (rows, rows), 1)
        same = same & (key_at <= query_at)
    return jnp.concatenate([same] * group, axis=1)


def blocks_needed(kv_refs, segq_ref, rows):
    first = jnp.min(segq_ref[0])
    return [jnp.max(block_ids(ref, rows)) == first for ref in kv_refs]


def attend_fwd_kernel(kv_heads, group, blocks, q_ref, *refs):
    kv_refs = refs[:blocks]
    segq_ref, o_ref, lse_ref, m_s, l_s, acc_s = refs[blocks:]
    rows = q_ref.shape[0]
    needed = blocks_needed(kv_refs, segq_ref, rows)
    for h in range(kv_heads):
        qg = heads_down(q_ref[...], h * group, group) * jnp.asarray(HD**-0.5, BF)
        for k in range(blocks):

            def step(k=k):
                key = kv_refs[k][0, :rows, h * HD : (h + 1) * HD]
                val = kv_refs[k][0, :rows, (kv_heads + h) * HD : (kv_heads + h + 1) * HD]
                mask = block_mask(k, segq_ref, kv_refs[k], rows, group)
                scores = jnp.where(mask, nt(key, qg), NEG)
                top = jnp.max(scores, axis=0, keepdims=True)
                if k == 0:
                    probs = jnp.exp(scores - top)
                    m_s[...] = top
                    l_s[...] = jnp.sum(probs, axis=0, keepdims=True)
                    acc_s[...] = tn(val, probs.astype(BF))
                else:
                    new = jnp.maximum(m_s[...], top)
                    fix = jnp.exp(m_s[...] - new)
                    probs = jnp.exp(scores - new)
                    m_s[...] = new
                    l_s[...] = l_s[...] * fix + jnp.sum(probs, axis=0, keepdims=True)
                    acc_s[...] = acc_s[...] * fix + tn(val, probs.astype(BF))

            if k == 0:
                step()
            else:
                pl.when(needed[k])(step)
        out = (acc_s[...] / l_s[...]).T.astype(BF)
        for g in range(group):
            o_ref[:, (h * group + g) * HD : (h * group + g + 1) * HD] = out[
                g * rows : (g + 1) * rows
            ]
        lse_ref[0, h : h + 1, :] = m_s[...] + jnp.log(l_s[...])


def attend_bwd_kernel(kv_heads, group, blocks, *refs):
    q_ref, do_ref, o_ref, lse_ref, cos_ref, sin_ref = refs[:6]
    kv_refs = refs[6 : 6 + blocks]
    segq_ref, dq_ref, j_ref = refs[6 + blocks : 9 + blocks]
    dkv_refs = refs[9 + blocks : 9 + 2 * blocks]
    dq_s = refs[9 + 2 * blocks]
    rows = q_ref.shape[0]
    needed = blocks_needed(kv_refs, segq_ref, rows)
    ones = jnp.ones((8, HD), BF)
    for h in range(kv_heads):
        qg = heads_down(q_ref[...], h * group, group) * jnp.asarray(HD**-0.5, BF)
        dog = heads_down(do_ref[...], h * group, group)
        og = heads_down(o_ref[...], h * group, group)
        prod = dog.astype(F32) * og.astype(F32)
        high = prod.astype(BF)
        low = (prod - high.astype(F32)).astype(BF)
        delta = (nt(ones, high) + nt(ones, low))[0:1]
        lse = lse_ref[0, h : h + 1, :]
        key_at = slice(h * HD, (h + 1) * HD)
        val_at = slice((kv_heads + h) * HD, (kv_heads + h + 1) * HD)
        for k in range(blocks):

            def step(k=k):
                key = kv_refs[k][0, :rows, key_at]
                val = kv_refs[k][0, :rows, val_at]
                mask = block_mask(k, segq_ref, kv_refs[k], rows, group)
                probs = jnp.exp(jnp.where(mask, nt(key, qg), NEG) - lse)
                score_grad = (probs * (nt(val, dog) - delta)).astype(BF)
                kind = dkv_refs[k].dtype
                dkv_refs[k][0, :, key_at] = nn(score_grad, qg).astype(kind)
                dkv_refs[k][0, :, val_at] = nn(probs.astype(BF), dog).astype(kind)
                dq = tn(key, score_grad)
                dq_s[h] = dq if k == 0 else dq_s[h] + dq

            if k == 0:
                step()
            else:
                pl.when(needed[k])(step)

                @pl.when(jnp.logical_not(needed[k]))
                def _(k=k):
                    zero = jnp.zeros((rows, HD), dkv_refs[k].dtype)
                    dkv_refs[k][0, :, key_at] = zero
                    dkv_refs[k][0, :, val_at] = zero

    turned = [(dq_s[h] * (HD**-0.5)).T for h in range(kv_heads)]
    dq = jnp.concatenate(
        [t[g * rows : (g + 1) * rows] for t in turned for g in range(group)], axis=1
    )
    inner = dq * q_ref[...].astype(F32)
    total = inner[:, :128]
    for i in range(1, dq.shape[1] // 128):
        total = total + inner[:, i * 128 : (i + 1) * 128]
    j_ref[...] = total
    dq_ref[...] = turn(dq, cos_ref[...], -sin_ref[...]).astype(BF)


def attend_call(kernel, rows_in, seqs_in, kvs, segq, outs, scratch, name, behind):
    seqs, _, rows = segq.shape
    kv_heads = kvs[0].shape[2] // (2 * HD)
    group = rows_in[0].shape[1] // (HD * kv_heads)
    blocks = len(kvs)

    def spec(shape):
        if len(shape) == 2:
            return pl.BlockSpec((rows, shape[1]), lambda i, *_: (i, 0))
        return pl.BlockSpec((1,) + shape[1:], lambda i, *_: (i,) + (0,) * (len(shape) - 1))

    args = [*rows_in[:3], *seqs_in, *rows_in[3:], *kvs, segq]
    run = functools.partial(kernel, kv_heads, group, blocks)
    return pl.pallas_call(
        ordered(run, len(args), len(behind)),
        grid=(seqs,),
        in_specs=[spec(a.shape) for a in args] + [ANY] * len(behind),
        out_specs=[spec(shape) for shape, _ in outs],
        scratch_shapes=[pltpu.VMEM(shape, F32) for shape in scratch],
        out_shape=[jax.ShapeDtypeStruct(shape, kind) for shape, kind in outs],
        compiler_params=params(),
        cost_estimate=cost(0, 0),
        name=name,
    )(*args, *behind)


def attend_forward(q, kvs, segq, behind):
    seqs, _, rows = segq.shape
    kv_heads = kvs[0].shape[2] // (2 * HD)
    long = q.shape[1] // (HD * kv_heads) * rows
    return attend_call(
        attend_fwd_kernel, [q], [], kvs, segq,
        [(q.shape, BF), ((seqs, kv_heads, long), F32)],
        [(1, long), (1, long), (HD, long)], "attend_forward", behind,
    )


def attend_backward(q, do, o, lse, cos, sin, kvs, segq, behind):
    rows = segq.shape[2]
    kv_heads = kvs[0].shape[2] // (2 * HD)
    long = q.shape[1] // (HD * kv_heads) * rows
    shape = (kvs[0].shape[0], rows, kvs[0].shape[2])
    grads = [(shape, F32 if k == 0 else BF) for k in range(len(kvs))]
    return attend_call(
        attend_bwd_kernel, [q, do, o, cos, sin], [lse], kvs, segq,
        [(q.shape, BF), ((q.shape[0], 128), F32)] + grads,
        [(kv_heads, HD, long)], "attend_backward", behind,
    )


def turn_kernel(turned, pre_ref, cos_ref, sin_ref, out_ref):
    pre = pre_ref[...]
    out_ref[:, :turned] = turn(pre[:, :turned], cos_ref[...], sin_ref[...]).astype(BF)
    if turned < pre.shape[1]:
        out_ref[:, turned:] = pre[:, turned:].astype(BF)


def turn_rows(pre, cos, sin, turned):
    return pl.pallas_call(
        functools.partial(turn_kernel, turned),
        out_shape=jax.ShapeDtypeStruct(pre.shape, BF),
        compiler_params=pltpu.CompilerParams(vmem_limit_bytes=32 * 2**20),
        name="turn_rows",
    )(pre, cos, sin)


def flip(count, bit):
    return [(i, i ^ bit) for i in range(count)]


def idle(*others):
    return pl.pallas_call(
        nothing,
        out_shape=jax.ShapeDtypeStruct((8, 128), F32),
        in_specs=[ANY] * len(others),
        out_specs=ANY,
        cost_estimate=pl.CostEstimate(
            flops=25300000000, bytes_accessed=0, transcendentals=0
        ),
        name="idle",
    )(*others)


class Clock:
    def __init__(self):
        self.last = []

    def now(self, value):
        return after(value, idle(*self.last)) if self.last else value

    def did(self, *values):
        self.last = list(values)
        return values[0]

    def go(self, value):
        others = [other for other in self.last if other is not value]
        return self.did(after(value, *others)) if others else value


class Plan:
    def __init__(self):
        self.fsdp = lax.axis_size("fsdp")
        self.ctx = lax.axis_size("ctx")
        self.tp = lax.axis_size("tp")
        if self.tp != 4 or self.ctx != 4:
            raise ValueError("unsupported mesh")
        self.y = lax.axis_index("fsdp")
        self.z = lax.axis_index("ctx")
        self.t = lax.axis_index("tp")
        self.pairs = self.fsdp == 2
        self.parity = self.z % 2
        self.order = list(range(4))
        if self.pairs:
            base = 2 * (1 - self.y)
            self.order = [2 * self.y, 2 * self.y + 1, base + self.parity, base + 1 - self.parity]
        self.picks = jnp.stack([jnp.asarray(q ^ self.t, jnp.int32) for q in self.order])
        quarters = [self.t, self.t ^ 1, self.t ^ 2, self.t ^ 3]
        self.homes = jnp.stack([jnp.asarray(self.slot(q), jnp.int32) for q in quarters])
        quarters = [self.t, self.t ^ 2, self.t ^ 1, self.t ^ 3]
        self.slots = jnp.stack([jnp.asarray(self.slot(q), jnp.int32) for q in quarters])
        parity = jnp.asarray(self.parity, jnp.int32)
        zero = jnp.zeros((), jnp.int32)
        self.sides = jnp.stack([2 + parity, 3 - parity, zero, zero + 1])
        self.half = jnp.stack([parity])
        ends = (self.z == 0) | (self.z == 3)
        self.ends = jnp.stack([ends.astype(jnp.int32)])

    def slot(self, quarter):
        if not self.pairs:
            return quarter
        low = quarter % 2
        return jnp.where(quarter // 2 == self.y, low, 2 + (low ^ self.parity))


def lay_kernel(homes, *refs):
    out_ref, sems = refs[4:]
    rows, width = out_ref.shape[0], out_ref.shape[1] // 4
    copies = []
    for n in range(4):
        columns = pl.ds(pl.multiple_of(homes[n] * width, width), width)
        source = refs[n].at[pl.ds(pl.program_id(0) * rows, rows)]
        copies.append(pltpu.make_async_copy(source, out_ref.at[:, columns], sems.at[n]))
        copies[-1].start()
    for copy in copies:
        copy.wait()


GAIN_ROWS = 16


def with_gain(rows_in, gain):
    parts, rest = [], gain
    for _ in range(3):
        kept = lax.reduce_precision(rest, exponent_bits=8, mantissa_bits=7)
        parts.append(kept.astype(BF))
        rest = rest - kept
    below = jnp.stack(parts + [jnp.zeros_like(parts[0])] * (GAIN_ROWS - 3))
    return jnp.concatenate([rows_in, below], axis=0)


def lay_norm_kernel(picks, *refs):
    gain_refs = refs[4:8]
    out_ref, scale_ref = refs[-2:]
    width = refs[0].shape[1]
    squares = 0.0
    for ref in refs[:4]:
        values = ref[...].astype(F32)
        squares = squares + jnp.sum(values * values, axis=1, keepdims=True)
    scale = lax.rsqrt(squares / (4 * width) + EPS)
    scale_ref[...] = jnp.broadcast_to(scale, scale_ref.shape)
    for place in range(4):
        for which in range(4):

            @pl.when(picks[place] == which)
            def _(place=place, which=which):
                at = slice(place * width, (place + 1) * width)
                parts = gain_refs[which][...].astype(F32)
                gain = parts[0:1] + parts[1:2] + parts[2:3]
                out_ref[:, at] = (refs[which][...].astype(F32) * scale * gain).astype(BF)


def lay_norm(plan, held, behind):
    rows, width = held[0].shape[0] - GAIN_ROWS, held[0].shape[1]
    block = min(rows, 256)
    part = pl.BlockSpec((block, width), lambda i, *_: (i, 0))
    below = pl.BlockSpec((GAIN_ROWS, width), lambda i, *_: (rows // GAIN_ROWS, 0))
    return pl.pallas_call(
        ordered_after_scalars(lay_norm_kernel, 8, len(behind)),
        grid_spec=pltpu.PrefetchScalarGridSpec(
            num_scalar_prefetch=1,
            grid=(rows // block,),
            in_specs=[part] * 4 + [below] * 4 + [ANY] * len(behind),
            out_specs=[
                pl.BlockSpec((block, 4 * width), lambda i, *_: (i, 0)),
                pl.BlockSpec((block, 128), lambda i, *_: (i, 0)),
            ],
        ),
        out_shape=[
            jax.ShapeDtypeStruct((rows, 4 * width), BF),
            jax.ShapeDtypeStruct((rows, 128), F32),
        ],
        compiler_params=params(),
        cost_estimate=cost(0, 0),
        name="lay_norm",
    )(plan.picks, *held, *held, *behind)


def lay(plan, held, behind):
    rows, width = held[0].shape
    block = 256

    def run(homes, *refs):
        lay_kernel(homes, *refs[:4], *refs[4 + len(behind) :])

    return pl.pallas_call(
        run,
        grid_spec=pltpu.PrefetchScalarGridSpec(
            num_scalar_prefetch=1,
            grid=(rows // block,),
            in_specs=[ANY] * (4 + len(behind)),
            out_specs=pl.BlockSpec((block, 4 * width), lambda i, *_: (i, 0)),
            scratch_shapes=[pltpu.SemaphoreType.DMA((4,))],
        ),
        out_shape=jax.ShapeDtypeStruct((rows, 4 * width), BF),
        compiler_params=params(),
        cost_estimate=cost(0, 0),
        name="lay",
    )(plan.homes, *held, *behind)


def blank(shape, kind):
    return pl.pallas_call(
        nothing, out_shape=jax.ShapeDtypeStruct(shape, kind), out_specs=ANY, name="blank"
    )()


def place(whole, part, *starts):
    return lax.dynamic_update_slice(whole, part.astype(whole.dtype), starts)


def ordered(kernel, count, extra):
    def run(*refs):
        kernel(*refs[:count], *refs[count + extra :])

    return run


def params(megabytes=60):
    return pltpu.CompilerParams(vmem_limit_bytes=megabytes * 2**20)


def cost(flops, size):
    return pl.CostEstimate(flops=1100000000, bytes_accessed=0, transcendentals=0)


def gate_up(j, gained, scale, segments, span, behind):
    rows = gained.shape[0]
    tile = span // 2
    starts = [k for k, _, _, _ in segments]

    def kernel(*refs):
        gained_ref, scale_ref = refs[:2]
        weights = refs[2 : 2 + 2 * len(segments)]
        raw_ref, act_ref = refs[2 + 2 * len(segments) :]
        raws = []
        for side in range(2):
            total = None
            for n, k in enumerate(starts):
                ref = weights[2 * n + side]
                term = nn(gained_ref[:, k : k + ref.shape[0]], ref[...])
                total = term if total is None else total + term
            raws.append(total)
        raw_ref[:, :tile] = raws[0]
        raw_ref[:, tile:] = raws[1]
        gate = raws[0] * scale_ref[...]
        act_ref[...] = (gate * jax.nn.sigmoid(gate) * (raws[1] * scale_ref[...])).astype(BF)

    args, specs = [gained, scale], [
        pl.BlockSpec(gained.shape, lambda i: (0, 0)),
        pl.BlockSpec(scale.shape, lambda i: (0, 0)),
    ]
    for _, size, arrays, at in segments:
        for side in range(2):
            args.append(arrays[side])
            specs.append(pl.BlockSpec((size, tile), lambda i, side=side, at=at: (0, at(i)[side])))
    return pl.pallas_call(
        ordered(kernel, len(args), len(behind)),
        grid=(2,),
        in_specs=specs + [ANY] * len(behind),
        out_specs=[
            pl.BlockSpec((rows, 2 * tile), lambda i: (0, i)),
            pl.BlockSpec((rows, tile), lambda i: (0, i)),
        ],
        out_shape=[
            jax.ShapeDtypeStruct((rows, 2 * span), F32),
            jax.ShapeDtypeStruct((rows, span), BF),
        ],
        compiler_params=params(),
        cost_estimate=cost(4 * rows * gained.shape[1] * span, 14 * 2**20),
        name="gate_up",
    )(*args, *behind)


def gate_up_back(j, cot, scale, raw, segments, span, behind):
    rows = cot.shape[0]
    tile = span // 2
    starts = [k for k, _, _, _ in segments]

    def kernel(*refs):
        cot_ref, scale_ref, raw_ref = refs[:3]
        weights = refs[3 : 3 + len(segments)]
        grad_ref, inner_ref = refs[3 + len(segments) :]
        total = None
        for n, k in enumerate(starts):
            ref = weights[n]
            term = nt(cot_ref[:, k : k + ref.shape[1]], ref[...])
            total = term if total is None else total + term
        scale_rows = scale_ref[...]
        act_grad = total * scale_rows
        gate_raw, up_raw = raw_ref[:, :tile], raw_ref[:, tile:]
        gate, up = gate_raw * scale_rows, up_raw * scale_rows
        sig = jax.nn.sigmoid(gate)
        gate_grad = (act_grad * up * sig * (1.0 + gate * (1.0 - sig))).astype(BF)
        up_grad = (act_grad * gate * sig).astype(BF)
        grad_ref[:, :tile] = gate_grad
        grad_ref[:, tile:] = up_grad
        inner = gate_grad.astype(F32) * gate_raw + up_grad.astype(F32) * up_raw
        part = inner[:, :128]
        for c in range(1, tile // 128):
            part = part + inner[:, c * 128 : (c + 1) * 128]

        @pl.when(pl.program_id(0) == 0)
        def _():
            inner_ref[...] = part

        @pl.when(pl.program_id(0) > 0)
        def _():
            inner_ref[...] += part

    args = [cot, scale, raw]
    specs = [
        pl.BlockSpec(cot.shape, lambda i: (0, 0)),
        pl.BlockSpec(scale.shape, lambda i: (0, 0)),
        pl.BlockSpec((rows, 2 * tile), lambda i: (0, i)),
    ]
    for _, size, array, at in segments:
        args.append(array)
        specs.append(pl.BlockSpec((tile, size), lambda i, at=at: (at(i), 0)))
    return pl.pallas_call(
        ordered(kernel, len(args), len(behind)),
        grid=(2,),
        in_specs=specs + [ANY] * len(behind),
        out_specs=[
            pl.BlockSpec((rows, 2 * tile), lambda i: (0, i)),
            pl.BlockSpec((rows, 128), lambda i: (0, 0)),
        ],
        out_shape=[
            jax.ShapeDtypeStruct((rows, 2 * span), BF),
            jax.ShapeDtypeStruct((rows, 128), F32),
        ],
        compiler_params=params(),
        cost_estimate=cost(2 * rows * cot.shape[1] * span, 12 * 2**20),
        name="gate_up_back",
    )(*args, *behind)


def back_to_width(grads, w_gate, w_up, near, far, span, behind):
    rows = grads[0].shape[0]
    parts, tile, steps = len(grads), span // 2, 4
    own, other = w_gate.shape[0] // steps, near[0].shape[0] // steps

    def kernel(*refs):
        grad_refs = refs[:parts]
        gate_ref, up_ref = refs[parts : parts + 2]
        near_refs = refs[parts + 2 : 2 * parts + 2]
        far_refs = refs[2 * parts + 2 : 3 * parts + 2]
        own_ref, near_out, far_out = refs[3 * parts + 2 :]
        own_sum, other_sum = None, None
        for j in range(parts):
            both = jnp.concatenate([near_refs[j][...], far_refs[j][...]], axis=0)
            term = nt(grad_refs[j][...], both)
            other_sum = term if j == 0 else other_sum + term
            for i in range(2):
                at = slice(j * span + i * tile, j * span + (i + 1) * tile)
                base = 2 * i * tile
                term = nt(grad_refs[j][:, base : base + tile], gate_ref[:, at])
                term = term + nt(grad_refs[j][:, base + tile : base + 2 * tile], up_ref[:, at])
                own_sum = term if own_sum is None else own_sum + term
        own_ref[...] = own_sum.astype(BF)
        near_out[...] = other_sum[:, :other].astype(BF)
        far_out[...] = other_sum[:, other:].astype(BF)

    args = list(grads) + [w_gate, w_up] + list(near) + list(far)
    specs = [pl.BlockSpec(g.shape, lambda i: (0, 0)) for g in grads]
    specs += [pl.BlockSpec((own, w_gate.shape[1]), lambda i: (i, 0))] * 2
    specs += [pl.BlockSpec((other, 2 * span), lambda i: (i, 0))] * (2 * parts)
    return pl.pallas_call(
        ordered(kernel, len(args), len(behind)),
        grid=(steps,),
        in_specs=specs + [ANY] * len(behind),
        out_specs=[
            pl.BlockSpec((rows, own), lambda i: (0, i)),
            pl.BlockSpec((rows, other), lambda i: (0, i)),
            pl.BlockSpec((rows, other), lambda i: (0, i)),
        ],
        out_shape=[
            jax.ShapeDtypeStruct((rows, n * steps), BF) for n in (own, other, other)
        ],
        compiler_params=params(),
        cost_estimate=cost(16 * rows * 2 * own * steps * span, 30 * 2**20),
        name="back_to_width",
    )(*args, *behind)


def down(acts, w_down, near, far, span, behind):
    rows = acts[0].shape[0]
    parts, steps = len(acts), 4
    own, other = w_down.shape[1] // steps, near[0].shape[1] // steps

    def kernel(*refs):
        act_refs = refs[:parts]
        down_ref = refs[parts]
        near_refs = refs[parts + 1 : 2 * parts + 1]
        far_refs = refs[2 * parts + 1 : 3 * parts + 1]
        own_ref, near_out, far_out = refs[3 * parts + 1 :]
        own_sum, other_sum = None, None
        for j in range(parts):
            both = jnp.concatenate([near_refs[j][...], far_refs[j][...]], axis=1)
            act = act_refs[j][...]
            other_term = nn(act, both)
            own_term = nn(act, down_ref[j * span : (j + 1) * span])
            other_sum = other_term if j == 0 else other_sum + other_term
            own_sum = own_term if j == 0 else own_sum + own_term
        own_ref[...] = own_sum.astype(BF)
        near_out[...] = other_sum[:, :other].astype(BF)
        far_out[...] = other_sum[:, other:].astype(BF)

    per = parts // len(near)
    args = list(acts) + [w_down]
    specs = [pl.BlockSpec(a.shape, lambda i: (0, 0)) for a in acts]
    specs += [pl.BlockSpec((w_down.shape[0], own), lambda i: (0, i))]
    for side in (near, far):
        for j in range(parts):
            args.append(side[j // per])
            specs.append(pl.BlockSpec((span, other), lambda i, j=j: (j % per, i)))
    return pl.pallas_call(
        ordered(kernel, len(args), len(behind)),
        grid=(steps,),
        in_specs=specs + [ANY] * len(behind),
        out_specs=[
            pl.BlockSpec((rows, own), lambda i: (0, i)),
            pl.BlockSpec((rows, other), lambda i: (0, i)),
            pl.BlockSpec((rows, other), lambda i: (0, i)),
        ],
        out_shape=[
            jax.ShapeDtypeStruct((rows, n * steps), BF) for n in (own, other, other)
        ],
        compiler_params=params(),
        cost_estimate=cost(8 * rows * own * steps * 2 * span, 20 * 2**20),
        name="down",
    )(*args, *behind)


def split_terms(plan, pieces, behind):
    rows = pieces[0].shape[0]
    width = sum(p.shape[1] for p in pieces) // 4
    block = 256
    homes = [(n, c) for n, p in enumerate(pieces) for c in range(p.shape[1] // width)]

    def kernel(slots, *refs):
        outs = refs[len(pieces) :]
        for q in range(4):
            for slot in range(4):

                @pl.when(slots[q] == slot)
                def _(q=q, slot=slot):
                    n, c = homes[slot]
                    at = slice((q % 2) * width, (q % 2 + 1) * width)
                    outs[q // 2][:, at] = refs[n][:, c * width : (c + 1) * width]

    return pl.pallas_call(
        ordered_after_scalars(kernel, len(pieces), len(behind)),
        grid_spec=pltpu.PrefetchScalarGridSpec(
            num_scalar_prefetch=1,
            grid=(rows // block,),
            in_specs=[pl.BlockSpec((block, p.shape[1]), lambda i, *_: (i, 0)) for p in pieces]
            + [ANY] * len(behind),
            out_specs=[pl.BlockSpec((block, 2 * width), lambda i, *_: (i, 0))] * 2,
        ),
        out_shape=[jax.ShapeDtypeStruct((rows, 2 * width), BF)] * 2,
        compiler_params=params(),
        cost_estimate=cost(rows, 16 * rows * width),
        name="split_terms",
    )(plan.slots, *pieces, *behind)


def ordered_after_scalars(kernel, count, extra):
    def run(scalars, *refs):
        kernel(scalars, *refs[:count], *refs[count + extra :])

    return run


def branch_terms(plan, attended, pieces, behind):
    rows = attended.shape[0]
    width = sum(p.shape[1] for p in pieces) // 4
    block = 256
    homes = [(n, c) for n, p in enumerate(pieces) for c in range(p.shape[1] // width)]

    def kernel(slots, att_ref, *refs):
        outs = refs[len(pieces) :]
        for q in range(4):
            for slot in range(4):

                @pl.when(slots[q] == slot)
                def _(q=q, slot=slot):
                    n, c = homes[slot]
                    at = slice((q % 2) * width, (q % 2 + 1) * width)
                    product = nn(att_ref[...], refs[n][:, c * width : (c + 1) * width])
                    outs[q // 2][:, at] = product.astype(BF)

    return pl.pallas_call(
        ordered_after_scalars(kernel, 1 + len(pieces), len(behind)),
        grid_spec=pltpu.PrefetchScalarGridSpec(
            num_scalar_prefetch=1,
            grid=(rows // block,),
            in_specs=[pl.BlockSpec((block, attended.shape[1]), lambda i, *_: (i, 0))]
            + [pl.BlockSpec(p.shape, lambda i, *_: (0, 0)) for p in pieces]
            + [ANY] * len(behind),
            out_specs=[pl.BlockSpec((block, 2 * width), lambda i, *_: (i, 0))] * 2,
        ),
        out_shape=[jax.ShapeDtypeStruct((rows, 2 * width), BF)] * 2,
        compiler_params=params(),
        cost_estimate=cost(0, 0),
        name="branch_terms",
    )(plan.slots, attended, *pieces, *behind)


def outer(left, right, slots, axis, folded, behind):
    rows = left.shape[0]
    if axis == 0:
        width, wide = left.shape[1] // 4, right.shape[1]
        in_specs = [
            pl.BlockSpec((rows, width), lambda i, slots: (0, slots[i])),
            pl.BlockSpec((rows, wide), lambda i, slots: (0, 0)),
        ]
    else:
        width, wide = left.shape[1], right.shape[1] // 4
        in_specs = [
            pl.BlockSpec((rows, width), lambda i, slots: (0, 0)),
            pl.BlockSpec((rows, wide), lambda i, slots: (0, slots[i])),
        ]
    beside = folded or axis == 1
    shape = (width, 2 * wide) if beside else (2 * width, wide)

    def first(i, slots):
        at = jnp.minimum(i, 1)
        return (0, at) if beside else (at, 0)

    def last(i, slots):
        at = jnp.maximum(i - 2, 0)
        return (0, at) if beside else (at, 0)

    def kernel(slots_ref, left_ref, right_ref, first_ref, last_ref):
        made = tn(left_ref[...], right_ref[...]).astype(BF)

        @pl.when(pl.program_id(0) < 2)
        def _():
            first_ref[...] = made

        @pl.when(pl.program_id(0) >= 2)
        def _():
            last_ref[...] = made

    return pl.pallas_call(
        ordered_after_scalars(kernel, 2, len(behind)),
        grid_spec=pltpu.PrefetchScalarGridSpec(
            num_scalar_prefetch=1,
            grid=(4,),
            in_specs=in_specs + [ANY] * len(behind),
            out_specs=[pl.BlockSpec((width, wide), first), pl.BlockSpec((width, wide), last)],
        ),
        out_shape=[jax.ShapeDtypeStruct(shape, BF)] * 2,
        compiler_params=params(),
        cost_estimate=cost(4 * rows * shape[0] * shape[1], 8 * 2**20),
        name="outer",
    )(slots, left, right, *behind)


def rows_spec(block, columns, first=0):
    return pl.BlockSpec((block, columns), lambda i, *_: (first // block + i, 0))


STEPS = 2


def part_shape(arrays, part):
    return (part.rows, arrays[0].shape[1]) if part is not None else arrays[0].shape


def enter(plan, part, ready, behind):
    arrays, specs = [], []
    if part is not None:
        arrays += [part.grad.own, part.grad.sent]
    if ready is not None:
        arrays += [ready.pair, ready.got]
    rows, columns = part_shape(arrays, part)
    block = rows // STEPS
    for n, array in enumerate(arrays):
        first = part.first if part is not None and n < 2 else 0
        specs.append(rows_spec(block, columns, first))

    def kernel(ends, *refs):
        given, results = refs[: len(arrays)], refs[len(arrays) :]
        sums = [
            (given[n][...].astype(F32) + given[n + 1][...].astype(F32)).astype(BF)
            for n in range(0, len(arrays), 2)
        ]
        results[0][...] = sums[0]
        if len(sums) == 2:
            results[1][...] = jnp.where(ends[0] != 0, sums[0], sums[1])

    count = len(arrays) // 2
    made = pl.pallas_call(
        ordered_after_scalars(kernel, len(arrays), len(behind)),
        grid_spec=pltpu.PrefetchScalarGridSpec(
            num_scalar_prefetch=1,
            grid=(STEPS,),
            in_specs=specs + [ANY] * len(behind),
            out_specs=[rows_spec(block, columns)] * count,
        ),
        out_shape=[jax.ShapeDtypeStruct((rows, columns), BF)] * count,
        compiler_params=params(),
        cost_estimate=cost(rows * columns, 6 * rows * columns * count),
        name="enter",
    )(plan.ends, *arrays, *behind)
    return made if count == 2 else (made[0], made[0])


def leave(plan, outs, term, there, got, writes, behind):
    rows, columns = got.shape
    block = rows // STEPS
    args, specs, shapes, out_specs, alias = [got], [], [], [], {}
    if term is not None:
        args.append(term)
        shapes.append(jax.ShapeDtypeStruct((rows, columns), BF))
        out_specs.append(rows_spec(block, columns))
    if writes is not None:
        args.append(there)
    specs = [rows_spec(block, columns)] * len(args)
    reads = len(args)
    for name, shape, wide, row, column, _ in writes or []:
        if name in outs:
            alias[1 + len(args)] = len(shapes)
            args.append(outs[name])
            specs.append(ANY)
        shapes.append(jax.ShapeDtypeStruct(shape, F32))
        out_specs.append(
            pl.BlockSpec((block, wide), lambda i, *_, r=row // block, c=column // wide: (r + i, c))
        )
    given = len(args)

    def kernel(ends, *refs):
        results = list(refs[given + len(behind) :])
        arrived = refs[0][...]
        if term is not None:
            total = refs[1][...].astype(F32) + arrived.astype(F32)
            results.pop(0)[...] = total.astype(BF)
        if writes is not None:
            total = jnp.where(ends[0] != 0, arrived, refs[reads - 1][...]).astype(F32)
            for out, (_, _, _, _, _, takes) in zip(results, writes):
                done = 0
                for start, size in takes:
                    out[:, done : done + size] = total[:, start : start + size]
                    done += size

    made = pl.pallas_call(
        kernel,
        grid_spec=pltpu.PrefetchScalarGridSpec(
            num_scalar_prefetch=1,
            grid=(STEPS,),
            in_specs=specs + [ANY] * len(behind),
            out_specs=out_specs,
        ),
        out_shape=shapes,
        input_output_aliases=alias,
        compiler_params=params(),
        cost_estimate=cost(rows * columns, 10 * rows * columns),
        name="leave",
    )(plan.ends, *args, *behind)
    made = list(made)
    first = made[0]
    pair = made.pop(0) if term is not None else None
    for (name, *_), value in zip(writes or [], made):
        outs[name] = value
    return pair, first


def take(plan, blocks, axis, behind):
    part = blocks[0][0].shape[axis] // 2
    sizes = [size for _, size, _ in blocks]

    def kernel(half, *refs):
        out_ref = refs[-1]
        at = 0
        for ref, size in zip(refs, sizes):
            if axis == 0:
                out_ref[:, at : at + size] = ref[...]
            else:
                out_ref[at : at + size] = ref[...]
            at += size

    specs = []
    for _, size, first in blocks:
        if axis == 0:
            spec = pl.BlockSpec((part, size), lambda i, half, first=first: (half[0], first))
        else:
            spec = pl.BlockSpec((size, part), lambda i, half, first=first: (first, half[0]))
        specs.append(spec)
    shape = (part, sum(sizes)) if axis == 0 else (sum(sizes), part)
    return pl.pallas_call(
        ordered_after_scalars(kernel, len(blocks), len(behind)),
        grid_spec=pltpu.PrefetchScalarGridSpec(
            num_scalar_prefetch=1,
            grid=(1,),
            in_specs=specs + [ANY] * len(behind),
            out_specs=pl.BlockSpec(shape, lambda i, half: (0, 0)),
        ),
        out_shape=jax.ShapeDtypeStruct(shape, BF),
        compiler_params=params(),
        cost_estimate=cost(0, 4 * shape[0] * shape[1]),
        name="take",
    )(plan.half, *[array for array, _, _ in blocks], *behind)


def project(rows_in, sides, cos, sin, ids, behind):
    rows, depth = rows_in.shape
    block = ids.shape[2]
    arrays = [array for pieces, _ in sides for _, side in pieces for array in side]
    widths = [sum(array.shape[1] for array in pieces[0][1]) for pieces, _ in sides]

    def kernel(*refs):
        in_ref, cos_ref, sin_ref, ids_ref = refs[:4]
        weights = refs[4 : 4 + len(arrays)]
        results = refs[4 + len(arrays) :]
        below = jnp.broadcast_to(ids_ref[0].astype(F32), (ID_ROWS, block)).astype(BF)
        results[0][block:, :block] = below
        at = 0
        for (pieces, turned), wide, out_ref in zip(sides, widths, results):
            total = None
            for first, side in pieces:
                values = [weights[at + n][...] for n in range(len(side))]
                at += len(side)
                value = values[0] if len(values) == 1 else jnp.concatenate(values, axis=1)
                term = nn(in_ref[:, first : first + value.shape[0]], value)
                total = term if total is None else total + term
            turned_part = turn(total[:, :turned], cos_ref[...], sin_ref[...])
            out_ref[:block, :turned] = turned_part.astype(BF)
            if turned < wide:
                out_ref[:block, turned:] = total[:, turned:].astype(BF)

    def of_rows(columns):
        return pl.BlockSpec((block, columns), lambda i: (i, 0))

    args = [rows_in, cos, sin, ids] + arrays
    specs = [of_rows(depth), of_rows(128), of_rows(128)]
    specs.append(pl.BlockSpec((1, 1, block), lambda i: (i, 0, 0)))
    specs += [pl.BlockSpec(a.shape, lambda i: (0, 0)) for a in arrays]
    steps = rows // block
    shapes = [(block + ID_ROWS * (n == 0), wide) for n, wide in enumerate(widths)]
    return pl.pallas_call(
        ordered(kernel, len(args), len(behind)),
        grid=(steps,),
        in_specs=specs + [ANY] * len(behind),
        out_specs=[pl.BlockSpec(shape, lambda i: (i, 0)) for shape in shapes],
        out_shape=[jax.ShapeDtypeStruct((steps * r, wide), BF) for r, wide in shapes],
        compiler_params=params(),
        cost_estimate=cost(0, 0),
        name="project",
    )(*args, *behind)


def back_projected(sides, behind):
    rows = sides[0][0].shape[0]
    count = len(sides[0][1])
    block = 256
    args = [s[0] for s in sides] + [a for s in sides for piece in s[1] for a in piece]

    def kernel(*refs):
        given, outs = refs[: len(args)], refs[len(args) :]
        totals = [None] * count
        at = len(sides)
        for k, (_, pieces) in enumerate(sides):
            for n, piece in enumerate(pieces):
                first = 0
                for _ in piece:
                    weight = given[at][...]
                    at += 1
                    term = nt(given[k][:, first : first + weight.shape[1]], weight)
                    first += weight.shape[1]
                    totals[n] = term if totals[n] is None else totals[n] + term
        for out, total in zip(outs, totals):
            out[...] = total.astype(BF)

    def of_rows(columns):
        return pl.BlockSpec((block, columns), lambda i: (i, 0))

    specs = [of_rows(s[0].shape[1]) for s in sides]
    specs += [pl.BlockSpec(a.shape, lambda i: (0, 0)) for a in args[len(sides) :]]
    widths = [piece[0].shape[0] for piece in sides[0][1]]
    return pl.pallas_call(
        ordered(kernel, len(args), len(behind)),
        grid=(rows // block,),
        in_specs=specs + [ANY] * len(behind),
        out_specs=[of_rows(w) for w in widths],
        out_shape=[jax.ShapeDtypeStruct((rows, w), BF) for w in widths],
        compiler_params=params(),
        cost_estimate=cost(4 * rows * sum(widths) * 512, 8 * 2**20),
        name="back_projected",
    )(*args, *behind)


def heads_back(rows_in, pieces, behind):
    rows, depth = rows_in.shape
    wide = pieces[0].shape[0]
    block = 256

    def kernel(*refs):
        in_ref, out_ref = refs[0], refs[-1]
        at, total = 0, None
        for ref in refs[1:-1]:
            size = ref.shape[1]
            term = nt(in_ref[:, at : at + size], ref[...])
            total = term if total is None else total + term
            at += size
        out_ref[...] = total.astype(BF)

    return pl.pallas_call(
        ordered(kernel, 1 + len(pieces), len(behind)),
        grid=(rows // block,),
        in_specs=[pl.BlockSpec((block, depth), lambda i: (i, 0))]
        + [pl.BlockSpec(p.shape, lambda i: (0, 0)) for p in pieces]
        + [ANY] * len(behind),
        out_specs=pl.BlockSpec((block, wide), lambda i: (i, 0)),
        out_shape=jax.ShapeDtypeStruct((rows, wide), BF),
        compiler_params=params(),
        cost_estimate=cost(2 * rows * depth * wide, 6 * 2**20),
        name="heads_back",
    )(rows_in, *pieces, *behind)


class TensorGather:
    def __init__(self, part):
        self.part = part
        self.far = lax.ppermute(part, "tp", flip(4, 2))
        self.near = lax.ppermute(part, "tp", flip(4, 1))

    def relay(self, clock):
        self.far = clock.now(self.far)
        clock.did(self.far)
        self.far_near = lax.ppermute(self.far, "tp", flip(4, 1))

    def held(self):
        return [self.part, self.near, self.far, self.far_near]


class TensorScatter:
    def __init__(self, keep, send):
        self.keep = keep
        self.width = keep.shape[1] // 2
        self.got = lax.ppermute(send, "tp", flip(4, 1))

    def cross(self, clock):
        self.got = clock.now(self.got)
        keep, got = self.keep[:, self.width :], self.got[:, self.width :]
        far = clock.did((keep.astype(F32) + got.astype(F32)).astype(BF))
        self.far = lax.ppermute(far, "tp", flip(4, 2))

    def total(self, clock):
        far = clock.now(self.far)
        own = self.keep[:, : self.width].astype(F32) + self.got[:, : self.width].astype(F32)
        return own + far.astype(F32)


def tensor_total(values):
    values = values + lax.ppermute(values, "tp", flip(4, 1))
    return values + lax.ppermute(values, "tp", flip(4, 2))


class Weight:
    def __init__(self, plan, blocks, axis):
        self.plan, self.blocks, self.axis = plan, blocks, axis

    def take(self, clock):
        axis = self.axis
        if not self.plan.pairs:
            sent = [
                lax.slice_in_dim(array, first * size, (first + 1) * size, axis=1 - axis)
                for array, size, first in self.blocks
            ]
            sent = jnp.concatenate(sent, axis=1 - axis)
            self.out = lax.all_gather(sent, "fsdp", axis=axis, tiled=True)
            return
        self.sent = clock.did(take(self.plan, self.blocks, axis, clock.last))

    def start(self, clock):
        if self.plan.pairs:
            self.near = lax.ppermute(clock.go(self.sent), "fsdp", flip(2, 1))

    def relay(self, clock):
        if self.plan.pairs:
            self.near = clock.did(clock.now(self.near))
            self.far = lax.ppermute(self.near, "ctx", flip(4, 1))

    def arrive(self, clock):
        if self.plan.pairs:
            self.far = clock.did(clock.now(self.far))

    def pieces(self, own):
        return [own, self.near, self.far] if self.plan.pairs else [self.out]


class Grad:
    def __init__(self, plan, clock, left, right, axis, folded=False):
        self.away, self.own = outer(left, right, plan.sides, axis, folded, clock.last)
        clock.did(self.away)
        self.sent = None
        self.arrived = False


class Part:
    def __init__(self, grad, first, rows, writes):
        self.grad, self.first, self.rows, self.writes = grad, first, rows, writes


class Line:
    def __init__(self, plan, clock, outs):
        self.plan, self.clock, self.outs = plan, clock, outs
        self.waiting, self.crossing, self.sent = [], [], []
        self.leaving, self.flying, self.depth = [], [], 0

    def add(self, grad, parts):
        self.leaving.append(grad)
        self.waiting += [Part(grad, *part) for part in parts]
        self.kick()

    def kick(self):
        while self.leaving and len(self.flying) < self.depth:
            grad = self.leaving.pop(0)
            grad.sent = lax.ppermute(self.clock.go(grad.away), "fsdp", flip(2, 1))
            self.flying.append(grad)

    def step(self):
        plan, clock = self.plan, self.clock
        part = self.waiting.pop(0) if self.waiting else None
        if part is not None and not part.grad.arrived:
            grad = part.grad
            grad.sent = clock.did(clock.now(grad.sent))
            grad.arrived = True
            self.flying.remove(grad)
            self.kick()
        ready = None
        if len(self.crossing) > (1 if part is not None else 0):
            ready = self.crossing.pop(0)
        if part is not None or ready is not None:
            term, there = enter(plan, part, ready, clock.last)
            clock.did(there)
            got = lax.ppermute(there, "ctx", flip(4, 1))
            self.sent.append((part, term if part is not None else None, there, got, ready))
            keep = 1 if part is not None else 1
        else:
            keep = 0
        if len(self.sent) > keep:
            part, term, there, got, ready = self.sent.pop(0)
            writes = ready.writes if ready is not None else None
            pair, made = leave(plan, self.outs, term, there, got, writes, clock.last)
            clock.did(made)
            if part is not None:
                part.pair = pair
                part.got = lax.ppermute(pair, "ctx", [(1, 2), (2, 1)])
                self.crossing.append(part)

    def drain(self):
        while self.waiting or self.crossing or self.sent:
            self.step()


def earlier_blocks(rows):
    return [rows] + [
        lax.ppermute(rows, "ctx", [(i, i + k) for i in range(4 - k)]) for k in range(1, 4)
    ]


def on_device(
    tokens,
    segment_ids,
    positions,
    attn_gain,
    w_query,
    w_key,
    w_value,
    w_output,
    mlp_gain,
    w_gate,
    w_up,
    w_down,
    cotangent,
):
    plan = Plan()
    clock = Clock()
    outs = {}
    line = Line(plan, clock, outs)
    seqs, length, part_width = tokens.shape
    rows = seqs * length
    width = part_width * plan.tp
    quarter = width // 4
    kv_width = w_key.shape[1]
    heads_width = w_query.shape[1]
    hidden = w_gate.shape[1]
    span = hidden // SPLITS
    tile = span // 2
    half = hidden // 2
    token_rows = tokens.reshape(rows, part_width)
    cot_rows = cotangent.reshape(rows, part_width)

    kv_weight = Weight(plan, [(w_key, kv_width, 0), (w_value, kv_width, 0)], 0)
    q_weight = Weight(plan, [(w_query, heads_width, 0)], 0)
    o_weight = Weight(plan, [(w_output, heads_width, 0)], 1)
    gu_weights = [
        Weight(plan, [(w, tile, 2 * j + i) for i in range(2) for w in (w_gate, w_up)], 0)
        for j in range(SPLITS)
    ]
    down_weights = [Weight(plan, [(w_down, half, h)], 1) for h in range(2)]
    token_part = TensorGather(with_gain(token_rows, attn_gain))
    kv_weight.take(clock)
    kv_weight.start(clock)
    q_weight.take(clock)
    q_weight.start(clock)
    kv_weight.relay(clock)
    o_weight.take(clock)
    frequency = jnp.exp(jnp.arange(HD // 2, dtype=F32) * (-2.0 * math.log(THETA) / HD))
    turn_angle = positions.reshape(rows, 1).astype(F32) * frequency
    cos_half, sin_half = jnp.cos(turn_angle), jnp.sin(turn_angle)
    cos = after(jnp.concatenate([cos_half] * 4, axis=1))
    sin = after(jnp.concatenate([-sin_half, sin_half] * 2, axis=1))
    token_part.relay(clock)
    q_weight.relay(clock)
    o_weight.start(clock)
    gu_weights[0].take(clock)
    gu_weights[0].start(clock)
    normed, scale_attn = lay_norm(plan, token_part.held(), clock.last)
    scale_attn = scale_attn[:, :1]
    clock.did(normed)
    kv_weight.arrive(clock)
    q_weight.arrive(clock)

    def stack(weight, own):
        at, pieces = 0, []
        for piece in weight.pieces(own):
            side = piece if isinstance(piece, list) else [piece]
            pieces.append((at, side))
            at += side[0].shape[0]
        return pieces

    kv_pieces = stack(kv_weight, [w_key, w_value])
    q_pieces = stack(q_weight, w_query)
    segq = segment_ids[:, None, :]
    kv_own, query_rot = project(
        normed, [(kv_pieces, kv_width), (q_pieces, heads_width)], cos, sin, segq, clock.last
    )
    clock.did(kv_own)
    segq = segq.astype(F32)
    kv_blocks = earlier_blocks(kv_own.reshape(seqs, length + ID_ROWS, 2 * kv_width))
    cot_part = TensorGather(clock.go(cot_rows))
    gu_weights[1].take(clock)
    o_weight.relay(clock)
    gu_weights[1].start(clock)
    gu_weights[2].take(clock)
    gu_weights[3].take(clock)
    for n in range(1, 4):
        kv_blocks[n] = clock.did(clock.now(kv_blocks[n]))
    cot_part.relay(clock)
    attended, log_totals = attend_forward(query_rot, kv_blocks, segq, clock.last)
    clock.did(attended)
    o_weight.arrive(clock)
    o_pieces = o_weight.pieces(w_output)
    keep, away = branch_terms(plan, attended, o_pieces, clock.last)
    clock.did(away)
    mid_branch = TensorScatter(keep, away)
    mid_branch.cross(clock)
    gu_weights[0].relay(clock)
    gu_weights[2].start(clock)
    cot_all = clock.did(lay(plan, cot_part.held(), clock.last))
    gu_weights[1].relay(clock)
    gu_weights[3].start(clock)
    resid_mid = token_rows.astype(F32) + mid_branch.total(clock)
    gained_part = TensorGather(clock.did((resid_mid * mlp_gain).astype(BF)))
    square_sum = tensor_total(jnp.sum(resid_mid * resid_mid, axis=-1))
    scale_mlp = lax.rsqrt(square_sum / width + EPS)[:, None]
    for w in down_weights:
        w.take(clock)
    gu_weights[0].arrive(clock)
    gained_part.relay(clock)
    gu_weights[2].relay(clock)
    down_weights[0].start(clock)
    gained = clock.did(lay(plan, gained_part.held(), clock.last))

    def gu_segments(j):
        def at_block(i):
            return (2 * i, 2 * i + 1)

        weight = gu_weights[j]
        if not plan.pairs:
            return [(0, width, (weight.out, weight.out), at_block)]
        return [
            (0, 2 * quarter, (w_gate, w_up), lambda i: (2 * j + i, 2 * j + i)),
            (2 * quarter, quarter, (weight.near, weight.near), at_block),
            (3 * quarter, quarter, (weight.far, weight.far), at_block),
        ]

    per = SPLITS // 2

    def down_segments(j):
        weight = down_weights[j // per]

        def at_block(i):
            return 2 * (j % per) + i

        if not plan.pairs:
            return [(0, width, weight.out, at_block)]
        return [
            (0, 2 * quarter, w_down, lambda i: 2 * j + i),
            (2 * quarter, quarter, weight.near, at_block),
            (3 * quarter, quarter, weight.far, at_block),
        ]

    def finish(left, right, axis, parts):
        total = lax.psum_scatter(tn(left, right), "fsdp", scatter_dimension=axis, tiled=True)
        total = lax.psum(total, "ctx")
        for first, count, writes in parts:
            for name, shape, _, row, column, takes in writes:
                value = jnp.concatenate(
                    [total[first : first + count, at : at + size] for at, size in takes], axis=1
                )
                base = outs[name] if name in outs else jnp.zeros(shape, F32)
                outs[name] = place(base, value, row, column)

    def send(left, right, axis, parts, folded=False):
        if plan.pairs:
            line.add(Grad(plan, clock, left, right, axis, folded), parts)
        else:
            finish(left, right, axis, parts)

    raws, acts = [], []
    for j in range(SPLITS):
        if j > 0:
            gu_weights[j].arrive(clock)
        raw, act = gate_up(j, gained, scale_mlp, gu_segments(j), span, clock.last)
        raws.append(raw)
        acts.append(clock.did(act))
        own = w_down.shape[1]
        writes = [("down", w_down.shape, own, j * span, 0, [(0, own)])]
        send(act, cot_all, 1, [(0, span, writes)])
        if j == 0:
            gu_weights[3].relay(clock)
            down_weights[1].start(clock)
        if j == 1:
            down_weights[0].relay(clock)
            line.depth = 2
            line.kick()
        if j == 2:
            down_weights[1].relay(clock)
    down_weights[0].arrive(clock)
    gu_grads, inners = [], []

    def send_gu(j):
        share = w_gate.shape[0] // 2
        takes = [[(2 * i * tile + side * tile, tile) for i in range(2)] for side in range(2)]
        parts = []
        for r in range(2):
            writes = [
                (name, w_gate.shape, span, r * share, j * span, way)
                for name, way in zip(("gate", "up"), takes)
            ]
            parts.append((r * share, share, writes))
        send(gained, gu_grads[j], 0, parts)

    for j in range(SPLITS):
        if j == per:
            down_weights[1].arrive(clock)
        gu_grad, inner = gate_up_back(
            j, cot_all, scale_mlp, raws[j], down_segments(j), span, clock.last
        )
        clock.did(gu_grad)
        gu_grads.append(gu_grad)
        inners.append(inner)
        if j % 2 == 1:
            line.step()
    mid_inner = tensor_total(jnp.sum(sum(inners), axis=1))[:, None]
    send_gu(0)
    if plan.pairs:
        near = [w.near for w in gu_weights]
        far = [w.far for w in gu_weights]
        terms = back_to_width(gu_grads, w_gate, w_up, near, far, span, clock.last)
    else:
        terms = [sum(nt(clock.now(g), w.out) for g, w in zip(gu_grads, gu_weights)).astype(BF)]
    clock.did(terms[0])
    line.step()
    keep, away = split_terms(plan, terms, clock.last)
    clock.did(away)
    mid_scatter = TensorScatter(keep, away)
    mid_inner = clock.did(clock.now(mid_inner))
    send_gu(1)
    mid_scatter.cross(clock)
    line.step()
    send_gu(2)
    scaled_grad = mid_scatter.total(clock)
    mlp_gain_part = jnp.sum(scaled_grad * resid_mid, axis=0)
    resid_mid_grad = (
        cot_rows.astype(F32)
        + mlp_gain * scaled_grad
        - resid_mid * (scale_mlp * scale_mlp * mid_inner / width)
    )
    branch_part = TensorGather(clock.did(resid_mid_grad.astype(BF)))
    line.step()
    send_gu(3)
    branch_part.relay(clock)
    branch_grad = clock.did(lay(plan, branch_part.held(), clock.last))

    attended_grad = clock.did(heads_back(branch_grad, o_pieces, clock.last))
    line.step()
    query_grad, in_inner, *kv_terms = attend_backward(
        query_rot, attended_grad, attended, log_totals, cos, sin, kv_blocks, segq, clock.last
    )
    clock.did(query_grad)

    def hop(terms):
        return lax.ppermute(terms.astype(BF), "ctx", [(i, i - 1) for i in range(1, 4)])

    hopping = hop(kv_terms[3])
    line.step()
    line.step()
    shape = w_output.shape
    send(
        attended, branch_grad, 1,
        [(0, shape[0], [("output", shape, shape[1], 0, 0, [(0, shape[1])])])],
    )
    hopping = hop(kv_terms[2].astype(F32) + clock.did(clock.now(hopping)).astype(F32))
    line.step()

    def halves(name, array, columns, at, total):
        share, wide = array.shape[0] // 2, array.shape[1]
        if not plan.pairs:
            return [(name, array.shape, wide, 0, 0, [(at, wide)])]
        return [
            (name + str(r), (share, wide), wide, 0, 0, [(r * total + at, wide)]) for r in range(2)
        ]

    count = quarter if plan.pairs else w_query.shape[0]
    writes = halves("query", w_query, heads_width, 0, heads_width)
    send(normed, query_grad, 0, [(0, count, writes)], folded=True)
    hopping = hop(kv_terms[1].astype(F32) + clock.did(clock.now(hopping)).astype(F32))
    if plan.pairs:
        near = [w.near for w in down_weights]
        far = [w.far for w in down_weights]
        terms = down(acts, w_down, near, far, span, clock.last)
    else:
        terms = 0.0
        for j in range(SPLITS):
            at = slice((j % per) * span, (j % per + 1) * span)
            terms = terms + nn(acts[j], down_weights[j // per].out[at])
        terms = [terms.astype(BF)]
    clock.did(terms[0])
    line.step()
    kv_sum = kv_terms[0] + clock.did(clock.now(hopping)).astype(F32)
    own = kv_own.reshape(seqs, length + ID_ROWS, 2 * kv_width)[:, :length]
    kv_inner = jnp.sum(kv_sum * own.astype(F32), axis=2).reshape(rows)
    kv_sum = kv_sum.reshape(rows, 2 * kv_width)
    kv_grad = clock.did(turn_rows(kv_sum, cos, -sin, kv_width))
    in_inner = jnp.sum(in_inner, axis=1) + kv_inner
    in_inner = tensor_total(in_inner)[:, None]
    kv_wide = jnp.pad(kv_grad, ((0, 0), (0, heads_width - 2 * kv_width)))
    writes = halves("key", w_key, kv_width, 0, heads_width)
    writes += halves("value", w_value, kv_width, kv_width, heads_width)
    send(normed, kv_wide, 0, [(0, count, writes)], folded=True)
    line.step()
    sides = [
        (grads, [side for _, side in pieces])
        for grads, pieces in ((query_grad, q_pieces), (kv_grad, kv_pieces))
    ]
    in_sides = back_projected(sides, clock.last)
    clock.did(in_sides[0])
    keep, away = split_terms(plan, in_sides, clock.last)
    clock.did(away)
    in_scatter = TensorScatter(keep, away)
    in_inner = clock.did(clock.now(in_inner))
    line.step()
    in_scatter.cross(clock)
    keep, away = split_terms(plan, terms, clock.last)
    clock.did(away)
    out_scatter = TensorScatter(keep, away)
    line.step()
    normed_grad = in_scatter.total(clock)
    own_tokens = token_rows.astype(F32)
    attn_gain_part = jnp.sum(normed_grad * own_tokens * scale_attn, axis=0)
    input_grad = clock.did(
        resid_mid_grad
        + scale_attn * attn_gain * normed_grad
        - own_tokens * (scale_attn * scale_attn * in_inner / width)
    )
    out_scatter.cross(clock)
    line.step()
    gain_grads = clock.now(jnp.concatenate([attn_gain_part, mlp_gain_part]))
    if plan.pairs:
        got = lax.ppermute(gain_grads, "fsdp", flip(2, 1))
        output = clock.did((resid_mid + out_scatter.total(clock)).astype(BF))
        gain_grads = clock.did(gain_grads + clock.now(got))
        line.step()
        for bits in (1, 3):
            got = lax.ppermute(gain_grads, "ctx", flip(4, bits))
            line.step()
            gain_grads = clock.did(gain_grads + clock.now(got))
    else:
        output = (resid_mid + out_scatter.total(clock)).astype(BF)
        gain_grads = lax.psum(gain_grads, ("fsdp", "ctx"))
    line.drain()

    def joined(name):
        return jnp.concatenate([outs[name + "0"], outs[name + "1"]]) if plan.pairs else outs[name]

    shape = (seqs, length, part_width)
    return (
        output.reshape(shape),
        input_grad.reshape(shape),
        gain_grads[:part_width],
        joined("query"),
        joined("key"),
        joined("value"),
        outs["output"],
        gain_grads[part_width:],
        outs["gate"],
        outs["up"],
        outs["down"],
    )


def solution(mesh):
    rows = P("fsdp", "ctx", "tp")
    per_token = P("fsdp", "ctx")
    columns = P("fsdp", "tp")
    across = P("tp", "fsdp")
    gain = P("tp")
    return jax.shard_map(
        on_device,
        mesh=mesh,
        in_specs=(
            rows, per_token, per_token, gain, columns, columns, columns, across, gain,
            columns, columns, across, rows,
        ),
        out_specs=(
            rows, rows, gain, columns, columns, columns, across, gain, columns, columns, across,
        ),
        check_vma=False,
    )
```

```python
import functools
import math

import jax
import jax.numpy as jnp
from jax import lax
from jax.experimental import pallas as pl
from jax.experimental.pallas import tpu as pltpu
from jax.sharding import PartitionSpec as P

HQ = 32
KV = 8
HD = 64

THETA = 500000.0
EPS = 1e-05
NEG = -1e30
BF = jnp.bfloat16
F32 = jnp.float32
SPLITS = 4
ANY = pl.BlockSpec(memory_space=pl.ANY)


def nn(left, right):
    return jnp.dot(left, right, preferred_element_type=F32)


def tn(left, right):
    return lax.dot_general(left, right, (((0,), (0,)), ((), ())), preferred_element_type=F32)


def nt(left, right):
    return lax.dot_general(left, right, (((1,), (1,)), ((), ())), preferred_element_type=F32)


def nothing(*refs):
    pass


def after(value, *others):
    return pl.pallas_call(
        nothing,
        out_shape=jax.ShapeDtypeStruct(value.shape, value.dtype),
        in_specs=[ANY] * (1 + len(others)),
        out_specs=ANY,
        input_output_aliases={0: 0},
        name="after",
    )(value, *others)


def turn(rows, cos, sin):
    width = rows.shape[1]
    lane = lax.broadcasted_iota(jnp.int32, rows.shape, 1)
    other = jnp.where(
        lane % HD < HD // 2,
        pltpu.roll(rows, width - HD // 2, 1),
        pltpu.roll(rows, HD // 2, 1),
    )
    reps = width // 128
    return rows * jnp.concatenate([cos] * reps, axis=1) + other * jnp.concatenate(
        [sin] * reps, axis=1
    )


def heads_down(rows, first, count):
    return jnp.concatenate(
        [rows[:, (first + g) * HD : (first + g + 1) * HD] for g in range(count)], axis=0
    )


ID_ROWS = 16


def block_ids(kv_ref, rows):
    return kv_ref[0, rows : rows + ID_ROWS, :rows].astype(F32)[0:1]


def block_mask(k, segq_ref, kv_ref, rows, group):
    ids = jnp.broadcast_to(block_ids(kv_ref, rows), (8, rows))
    same = ids.T[:, 0:1] == segq_ref[0]
    if k == 0:
        key_at = lax.broadcasted_iota(jnp.int32, (rows, rows), 0)
        query_at = lax.broadcasted_iota(jnp.int32, (rows, rows), 1)
        same = same & (key_at <= query_at)
    return jnp.concatenate([same] * group, axis=1)


def blocks_needed(kv_refs, segq_ref, rows):
    first = jnp.min(segq_ref[0])
    return [jnp.max(block_ids(ref, rows)) == first for ref in kv_refs]


def attend_fwd_kernel(kv_heads, group, blocks, q_ref, *refs):
    kv_refs = refs[:blocks]
    segq_ref, o_ref, lse_ref, m_s, l_s, acc_s = refs[blocks:]
    rows = q_ref.shape[0]
    needed = blocks_needed(kv_refs, segq_ref, rows)
    for h in range(kv_heads):
        qg = heads_down(q_ref[...], h * group, group) * jnp.asarray(HD**-0.5, BF)
        for k in range(blocks):

            def step(k=k):
                key = kv_refs[k][0, :rows, h * HD : (h + 1) * HD]
                val = kv_refs[k][0, :rows, (kv_heads + h) * HD : (kv_heads + h + 1) * HD]
                mask = block_mask(k, segq_ref, kv_refs[k], rows, group)
                scores = jnp.where(mask, nt(key, qg), NEG)
                top = jnp.max(scores, axis=0, keepdims=True)
                if k == 0:
                    probs = jnp.exp(scores - top)
                    m_s[...] = top
                    l_s[...] = jnp.sum(probs, axis=0, keepdims=True)
                    acc_s[...] = tn(val, probs.astype(BF))
                else:
                    new = jnp.maximum(m_s[...], top)
                    fix = jnp.exp(m_s[...] - new)
                    probs = jnp.exp(scores - new)
                    m_s[...] = new
                    l_s[...] = l_s[...] * fix + jnp.sum(probs, axis=0, keepdims=True)
                    acc_s[...] = acc_s[...] * fix + tn(val, probs.astype(BF))

            if k == 0:
                step()
            else:
                pl.when(needed[k])(step)
        out = (acc_s[...] / l_s[...]).T.astype(BF)
        for g in range(group):
            o_ref[:, (h * group + g) * HD : (h * group + g + 1) * HD] = out[
                g * rows : (g + 1) * rows
            ]
        lse_ref[0, h : h + 1, :] = m_s[...] + jnp.log(l_s[...])


def attend_bwd_kernel(kv_heads, group, blocks, *refs):
    q_ref, do_ref, o_ref, lse_ref, cos_ref, sin_ref = refs[:6]
    kv_refs = refs[6 : 6 + blocks]
    segq_ref, dq_ref, j_ref = refs[6 + blocks : 9 + blocks]
    dkv_refs = refs[9 + blocks : 9 + 2 * blocks]
    dq_s = refs[9 + 2 * blocks]
    rows = q_ref.shape[0]
    needed = blocks_needed(kv_refs, segq_ref, rows)
    ones = jnp.ones((8, HD), BF)
    for h in range(kv_heads):
        qg = heads_down(q_ref[...], h * group, group) * jnp.asarray(HD**-0.5, BF)
        dog = heads_down(do_ref[...], h * group, group)
        og = heads_down(o_ref[...], h * group, group)
        prod = dog.astype(F32) * og.astype(F32)
        high = prod.astype(BF)
        low = (prod - high.astype(F32)).astype(BF)
        delta = (nt(ones, high) + nt(ones, low))[0:1]
        lse = lse_ref[0, h : h + 1, :]
        key_at = slice(h * HD, (h + 1) * HD)
        val_at = slice((kv_heads + h) * HD, (kv_heads + h + 1) * HD)
        for k in range(blocks):

            def step(k=k):
                key = kv_refs[k][0, :rows, key_at]
                val = kv_refs[k][0, :rows, val_at]
                mask = block_mask(k, segq_ref, kv_refs[k], rows, group)
                probs = jnp.exp(jnp.where(mask, nt(key, qg), NEG) - lse)
                score_grad = (probs * (nt(val, dog) - delta)).astype(BF)
                kind = dkv_refs[k].dtype
                dkv_refs[k][0, :, key_at] = nn(score_grad, qg).astype(kind)
                dkv_refs[k][0, :, val_at] = nn(probs.astype(BF), dog).astype(kind)
                dq = tn(key, score_grad)
                dq_s[h] = dq if k == 0 else dq_s[h] + dq

            if k == 0:
                step()
            else:
                pl.when(needed[k])(step)

                @pl.when(jnp.logical_not(needed[k]))
                def _(k=k):
                    zero = jnp.zeros((rows, HD), dkv_refs[k].dtype)
                    dkv_refs[k][0, :, key_at] = zero
                    dkv_refs[k][0, :, val_at] = zero

    turned = [(dq_s[h] * (HD**-0.5)).T for h in range(kv_heads)]
    dq = jnp.concatenate(
        [t[g * rows : (g + 1) * rows] for t in turned for g in range(group)], axis=1
    )
    inner = dq * q_ref[...].astype(F32)
    total = inner[:, :128]
    for i in range(1, dq.shape[1] // 128):
        total = total + inner[:, i * 128 : (i + 1) * 128]
    j_ref[...] = total
    dq_ref[...] = turn(dq, cos_ref[...], -sin_ref[...]).astype(BF)


def attend_call(kernel, rows_in, seqs_in, kvs, segq, outs, scratch, name, behind):
    seqs, _, rows = segq.shape
    kv_heads = kvs[0].shape[2] // (2 * HD)
    group = rows_in[0].shape[1] // (HD * kv_heads)
    blocks = len(kvs)

    def spec(shape):
        if len(shape) == 2:
            return pl.BlockSpec((rows, shape[1]), lambda i, *_: (i, 0))
        return pl.BlockSpec((1,) + shape[1:], lambda i, *_: (i,) + (0,) * (len(shape) - 1))

    args = [*rows_in[:3], *seqs_in, *rows_in[3:], *kvs, segq]
    run = functools.partial(kernel, kv_heads, group, blocks)
    return pl.pallas_call(
        ordered(run, len(args), len(behind)),
        grid=(seqs,),
        in_specs=[spec(a.shape) for a in args] + [ANY] * len(behind),
        out_specs=[spec(shape) for shape, _ in outs],
        scratch_shapes=[pltpu.VMEM(shape, F32) for shape in scratch],
        out_shape=[jax.ShapeDtypeStruct(shape, kind) for shape, kind in outs],
        compiler_params=params(),
        cost_estimate=cost(0, 0),
        name=name,
    )(*args, *behind)


def attend_forward(q, kvs, segq, behind):
    seqs, _, rows = segq.shape
    kv_heads = kvs[0].shape[2] // (2 * HD)
    long = q.shape[1] // (HD * kv_heads) * rows
    return attend_call(
        attend_fwd_kernel, [q], [], kvs, segq,
        [(q.shape, BF), ((seqs, kv_heads, long), F32)],
        [(1, long), (1, long), (HD, long)], "attend_forward", behind,
    )


def attend_backward(q, do, o, lse, cos, sin, kvs, segq, behind):
    rows = segq.shape[2]
    kv_heads = kvs[0].shape[2] // (2 * HD)
    long = q.shape[1] // (HD * kv_heads) * rows
    shape = (kvs[0].shape[0], rows, kvs[0].shape[2])
    grads = [(shape, F32 if k == 0 else BF) for k in range(len(kvs))]
    return attend_call(
        attend_bwd_kernel, [q, do, o, cos, sin], [lse], kvs, segq,
        [(q.shape, BF), ((q.shape[0], 128), F32)] + grads,
        [(kv_heads, HD, long)], "attend_backward", behind,
    )


def turn_kernel(turned, pre_ref, cos_ref, sin_ref, out_ref):
    pre = pre_ref[...]
    out_ref[:, :turned] = turn(pre[:, :turned], cos_ref[...], sin_ref[...]).astype(BF)
    if turned < pre.shape[1]:
        out_ref[:, turned:] = pre[:, turned:].astype(BF)


def turn_rows(pre, cos, sin, turned):
    return pl.pallas_call(
        functools.partial(turn_kernel, turned),
        out_shape=jax.ShapeDtypeStruct(pre.shape, BF),
        compiler_params=pltpu.CompilerParams(vmem_limit_bytes=32 * 2**20),
        name="turn_rows",
    )(pre, cos, sin)


def flip(count, bit):
    return [(i, i ^ bit) for i in range(count)]


def idle(*others):
    return pl.pallas_call(
        nothing,
        out_shape=jax.ShapeDtypeStruct((8, 128), F32),
        in_specs=[ANY] * len(others),
        out_specs=ANY,
        cost_estimate=pl.CostEstimate(
            flops=25300000000, bytes_accessed=0, transcendentals=0
        ),
        name="idle",
    )(*others)


class Clock:
    def __init__(self):
        self.last = []

    def now(self, value):
        return after(value, idle(*self.last)) if self.last else value

    def did(self, *values):
        self.last = list(values)
        return values[0]

    def go(self, value):
        others = [other for other in self.last if other is not value]
        return self.did(after(value, *others)) if others else value


class Plan:
    def __init__(self):
        self.fsdp = lax.axis_size("fsdp")
        self.ctx = lax.axis_size("ctx")
        self.tp = lax.axis_size("tp")
        if self.tp != 4 or self.ctx != 4:
            raise ValueError("unsupported mesh")
        self.y = lax.axis_index("fsdp")
        self.z = lax.axis_index("ctx")
        self.t = lax.axis_index("tp")
        self.pairs = self.fsdp == 2
        self.parity = self.z % 2
        self.order = list(range(4))
        if self.pairs:
            base = 2 * (1 - self.y)
            self.order = [2 * self.y, 2 * self.y + 1, base + self.parity, base + 1 - self.parity]
        self.picks = jnp.stack([jnp.asarray(q ^ self.t, jnp.int32) for q in self.order])
        quarters = [self.t, self.t ^ 1, self.t ^ 2, self.t ^ 3]
        self.homes = jnp.stack([jnp.asarray(self.slot(q), jnp.int32) for q in quarters])
        quarters = [self.t, self.t ^ 2, self.t ^ 1, self.t ^ 3]
        self.slots = jnp.stack([jnp.asarray(self.slot(q), jnp.int32) for q in quarters])
        parity = jnp.asarray(self.parity, jnp.int32)
        zero = jnp.zeros((), jnp.int32)
        self.sides = jnp.stack([2 + parity, 3 - parity, zero, zero + 1])
        self.half = jnp.stack([parity])
        ends = (self.z == 0) | (self.z == 3)
        self.ends = jnp.stack([ends.astype(jnp.int32)])

    def slot(self, quarter):
        if not self.pairs:
            return quarter
        low = quarter % 2
        return jnp.where(quarter // 2 == self.y, low, 2 + (low ^ self.parity))


def lay_kernel(homes, *refs):
    out_ref, sems = refs[4:]
    rows, width = out_ref.shape[0], out_ref.shape[1] // 4
    copies = []
    for n in range(4):
        columns = pl.ds(pl.multiple_of(homes[n] * width, width), width)
        source = refs[n].at[pl.ds(pl.program_id(0) * rows, rows)]
        copies.append(pltpu.make_async_copy(source, out_ref.at[:, columns], sems.at[n]))
        copies[-1].start()
    for copy in copies:
        copy.wait()


GAIN_ROWS = 16


def with_gain(rows_in, gain):
    parts, rest = [], gain
    for _ in range(3):
        kept = lax.reduce_precision(rest, exponent_bits=8, mantissa_bits=7)
        parts.append(kept.astype(BF))
        rest = rest - kept
    below = jnp.stack(parts + [jnp.zeros_like(parts[0])] * (GAIN_ROWS - 3))
    return jnp.concatenate([rows_in, below], axis=0)


def lay_norm_kernel(picks, *refs):
    gain_refs = refs[4:8]
    out_ref, scale_ref = refs[-2:]
    width = refs[0].shape[1]
    squares = 0.0
    for ref in refs[:4]:
        values = ref[...].astype(F32)
        squares = squares + jnp.sum(values * values, axis=1, keepdims=True)
    scale = lax.rsqrt(squares / (4 * width) + EPS)
    scale_ref[...] = jnp.broadcast_to(scale, scale_ref.shape)
    for place in range(4):
        for which in range(4):

            @pl.when(picks[place] == which)
            def _(place=place, which=which):
                at = slice(place * width, (place + 1) * width)
                parts = gain_refs[which][...].astype(F32)
                gain = parts[0:1] + parts[1:2] + parts[2:3]
                out_ref[:, at] = (refs[which][...].astype(F32) * scale * gain).astype(BF)


def lay_norm(plan, held, behind):
    rows, width = held[0].shape[0] - GAIN_ROWS, held[0].shape[1]
    block = min(rows, 256)
    part = pl.BlockSpec((block, width), lambda i, *_: (i, 0))
    below = pl.BlockSpec((GAIN_ROWS, width), lambda i, *_: (rows // GAIN_ROWS, 0))
    return pl.pallas_call(
        ordered_after_scalars(lay_norm_kernel, 8, len(behind)),
        grid_spec=pltpu.PrefetchScalarGridSpec(
            num_scalar_prefetch=1,
            grid=(rows // block,),
            in_specs=[part] * 4 + [below] * 4 + [ANY] * len(behind),
            out_specs=[
                pl.BlockSpec((block, 4 * width), lambda i, *_: (i, 0)),
                pl.BlockSpec((block, 128), lambda i, *_: (i, 0)),
            ],
        ),
        out_shape=[
            jax.ShapeDtypeStruct((rows, 4 * width), BF),
            jax.ShapeDtypeStruct((rows, 128), F32),
        ],
        compiler_params=params(),
        cost_estimate=cost(0, 0),
        name="lay_norm",
    )(plan.picks, *held, *held, *behind)


def lay(plan, held, behind):
    rows, width = held[0].shape
    block = 256

    def run(homes, *refs):
        lay_kernel(homes, *refs[:4], *refs[4 + len(behind) :])

    return pl.pallas_call(
        run,
        grid_spec=pltpu.PrefetchScalarGridSpec(
            num_scalar_prefetch=1,
            grid=(rows // block,),
            in_specs=[ANY] * (4 + len(behind)),
            out_specs=pl.BlockSpec((block, 4 * width), lambda i, *_: (i, 0)),
            scratch_shapes=[pltpu.SemaphoreType.DMA((4,))],
        ),
        out_shape=jax.ShapeDtypeStruct((rows, 4 * width), BF),
        compiler_params=params(),
        cost_estimate=cost(0, 0),
        name="lay",
    )(plan.homes, *held, *behind)


def blank(shape, kind):
    return pl.pallas_call(
        nothing, out_shape=jax.ShapeDtypeStruct(shape, kind), out_specs=ANY, name="blank"
    )()


def place(whole, part, *starts):
    return lax.dynamic_update_slice(whole, part.astype(whole.dtype), starts)


def ordered(kernel, count, extra):
    def run(*refs):
        kernel(*refs[:count], *refs[count + extra :])

    return run


def params(megabytes=60):
    return pltpu.CompilerParams(vmem_limit_bytes=megabytes * 2**20)


def cost(flops, size):
    return pl.CostEstimate(flops=1100000000, bytes_accessed=0, transcendentals=0)


def gate_up(j, gained, scale, segments, span, behind):
    rows = gained.shape[0]
    tile = span // 2
    starts = [k for k, _, _, _ in segments]

    def kernel(*refs):
        gained_ref, scale_ref = refs[:2]
        weights = refs[2 : 2 + 2 * len(segments)]
        raw_ref, act_ref = refs[2 + 2 * len(segments) :]
        raws = []
        for side in range(2):
            total = None
            for n, k in enumerate(starts):
                ref = weights[2 * n + side]
                term = nn(gained_ref[:, k : k + ref.shape[0]], ref[...])
                total = term if total is None else total + term
            raws.append(total)
        raw_ref[:, :tile] = raws[0]
        raw_ref[:, tile:] = raws[1]
        gate = raws[0] * scale_ref[...]
        act_ref[...] = (gate * jax.nn.sigmoid(gate) * (raws[1] * scale_ref[...])).astype(BF)

    args, specs = [gained, scale], [
        pl.BlockSpec(gained.shape, lambda i: (0, 0)),
        pl.BlockSpec(scale.shape, lambda i: (0, 0)),
    ]
    for _, size, arrays, at in segments:
        for side in range(2):
            args.append(arrays[side])
            specs.append(pl.BlockSpec((size, tile), lambda i, side=side, at=at: (0, at(i)[side])))
    return pl.pallas_call(
        ordered(kernel, len(args), len(behind)),
        grid=(2,),
        in_specs=specs + [ANY] * len(behind),
        out_specs=[
            pl.BlockSpec((rows, 2 * tile), lambda i: (0, i)),
            pl.BlockSpec((rows, tile), lambda i: (0, i)),
        ],
        out_shape=[
            jax.ShapeDtypeStruct((rows, 2 * span), F32),
            jax.ShapeDtypeStruct((rows, span), BF),
        ],
        compiler_params=params(),
        cost_estimate=cost(4 * rows * gained.shape[1] * span, 14 * 2**20),
        name="gate_up",
    )(*args, *behind)


def gate_up_back(j, cot, scale, raw, segments, span, behind):
    rows = cot.shape[0]
    tile = span // 2
    starts = [k for k, _, _, _ in segments]

    def kernel(*refs):
        cot_ref, scale_ref, raw_ref = refs[:3]
        weights = refs[3 : 3 + len(segments)]
        grad_ref, inner_ref = refs[3 + len(segments) :]
        total = None
        for n, k in enumerate(starts):
            ref = weights[n]
            term = nt(cot_ref[:, k : k + ref.shape[1]], ref[...])
            total = term if total is None else total + term
        scale_rows = scale_ref[...]
        act_grad = total * scale_rows
        gate_raw, up_raw = raw_ref[:, :tile], raw_ref[:, tile:]
        gate, up = gate_raw * scale_rows, up_raw * scale_rows
        sig = jax.nn.sigmoid(gate)
        gate_grad = (act_grad * up * sig * (1.0 + gate * (1.0 - sig))).astype(BF)
        up_grad = (act_grad * gate * sig).astype(BF)
        grad_ref[:, :tile] = gate_grad
        grad_ref[:, tile:] = up_grad
        inner = gate_grad.astype(F32) * gate_raw + up_grad.astype(F32) * up_raw
        part = inner[:, :128]
        for c in range(1, tile // 128):
            part = part + inner[:, c * 128 : (c + 1) * 128]

        @pl.when(pl.program_id(0) == 0)
        def _():
            inner_ref[...] = part

        @pl.when(pl.program_id(0) > 0)
        def _():
            inner_ref[...] += part

    args = [cot, scale, raw]
    specs = [
        pl.BlockSpec(cot.shape, lambda i: (0, 0)),
        pl.BlockSpec(scale.shape, lambda i: (0, 0)),
        pl.BlockSpec((rows, 2 * tile), lambda i: (0, i)),
    ]
    for _, size, array, at in segments:
        args.append(array)
        specs.append(pl.BlockSpec((tile, size), lambda i, at=at: (at(i), 0)))
    return pl.pallas_call(
        ordered(kernel, len(args), len(behind)),
        grid=(2,),
        in_specs=specs + [ANY] * len(behind),
        out_specs=[
            pl.BlockSpec((rows, 2 * tile), lambda i: (0, i)),
            pl.BlockSpec((rows, 128), lambda i: (0, 0)),
        ],
        out_shape=[
            jax.ShapeDtypeStruct((rows, 2 * span), BF),
            jax.ShapeDtypeStruct((rows, 128), F32),
        ],
        compiler_params=params(),
        cost_estimate=cost(2 * rows * cot.shape[1] * span, 12 * 2**20),
        name="gate_up_back",
    )(*args, *behind)


def back_to_width(grads, w_gate, w_up, near, far, span, behind):
    rows = grads[0].shape[0]
    parts, tile, steps = len(grads), span // 2, 4
    own, other = w_gate.shape[0] // steps, near[0].shape[0] // steps

    def kernel(*refs):
        grad_refs = refs[:parts]
        gate_ref, up_ref = refs[parts : parts + 2]
        near_refs = refs[parts + 2 : 2 * parts + 2]
        far_refs = refs[2 * parts + 2 : 3 * parts + 2]
        own_ref, near_out, far_out = refs[3 * parts + 2 :]
        own_sum, other_sum = None, None
        for j in range(parts):
            both = jnp.concatenate([near_refs[j][...], far_refs[j][...]], axis=0)
            term = nt(grad_refs[j][...], both)
            other_sum = term if j == 0 else other_sum + term
            for i in range(2):
                at = slice(j * span + i * tile, j * span + (i + 1) * tile)
                base = 2 * i * tile
                term = nt(grad_refs[j][:, base : base + tile], gate_ref[:, at])
                term = term + nt(grad_refs[j][:, base + tile : base + 2 * tile], up_ref[:, at])
                own_sum = term if own_sum is None else own_sum + term
        own_ref[...] = own_sum.astype(BF)
        near_out[...] = other_sum[:, :other].astype(BF)
        far_out[...] = other_sum[:, other:].astype(BF)

    args = list(grads) + [w_gate, w_up] + list(near) + list(far)
    specs = [pl.BlockSpec(g.shape, lambda i: (0, 0)) for g in grads]
    specs += [pl.BlockSpec((own, w_gate.shape[1]), lambda i: (i, 0))] * 2
    specs += [pl.BlockSpec((other, 2 * span), lambda i: (i, 0))] * (2 * parts)
    return pl.pallas_call(
        ordered(kernel, len(args), len(behind)),
        grid=(steps,),
        in_specs=specs + [ANY] * len(behind),
        out_specs=[
            pl.BlockSpec((rows, own), lambda i: (0, i)),
            pl.BlockSpec((rows, other), lambda i: (0, i)),
            pl.BlockSpec((rows, other), lambda i: (0, i)),
        ],
        out_shape=[
            jax.ShapeDtypeStruct((rows, n * steps), BF) for n in (own, other, other)
        ],
        compiler_params=params(),
        cost_estimate=cost(16 * rows * 2 * own * steps * span, 30 * 2**20),
        name="back_to_width",
    )(*args, *behind)


def down(acts, w_down, near, far, span, behind):
    rows = acts[0].shape[0]
    parts, steps = len(acts), 4
    own, other = w_down.shape[1] // steps, near[0].shape[1] // steps

    def kernel(*refs):
        act_refs = refs[:parts]
        down_ref = refs[parts]
        near_refs = refs[parts + 1 : 2 * parts + 1]
        far_refs = refs[2 * parts + 1 : 3 * parts + 1]
        own_ref, near_out, far_out = refs[3 * parts + 1 :]
        own_sum, other_sum = None, None
        for j in range(parts):
            both = jnp.concatenate([near_refs[j][...], far_refs[j][...]], axis=1)
            act = act_refs[j][...]
            other_term = nn(act, both)
            own_term = nn(act, down_ref[j * span : (j + 1) * span])
            other_sum = other_term if j == 0 else other_sum + other_term
            own_sum = own_term if j == 0 else own_sum + own_term
        own_ref[...] = own_sum.astype(BF)
        near_out[...] = other_sum[:, :other].astype(BF)
        far_out[...] = other_sum[:, other:].astype(BF)

    per = parts // len(near)
    args = list(acts) + [w_down]
    specs = [pl.BlockSpec(a.shape, lambda i: (0, 0)) for a in acts]
    specs += [pl.BlockSpec((w_down.shape[0], own), lambda i: (0, i))]
    for side in (near, far):
        for j in range(parts):
            args.append(side[j // per])
            specs.append(pl.BlockSpec((span, other), lambda i, j=j: (j % per, i)))
    return pl.pallas_call(
        ordered(kernel, len(args), len(behind)),
        grid=(steps,),
        in_specs=specs + [ANY] * len(behind),
        out_specs=[
            pl.BlockSpec((rows, own), lambda i: (0, i)),
            pl.BlockSpec((rows, other), lambda i: (0, i)),
            pl.BlockSpec((rows, other), lambda i: (0, i)),
        ],
        out_shape=[
            jax.ShapeDtypeStruct((rows, n * steps), BF) for n in (own, other, other)
        ],
        compiler_params=params(),
        cost_estimate=cost(8 * rows * own * steps * 2 * span, 20 * 2**20),
        name="down",
    )(*args, *behind)


def split_terms(plan, pieces, behind):
    rows = pieces[0].shape[0]
    width = sum(p.shape[1] for p in pieces) // 4
    block = 256
    homes = [(n, c) for n, p in enumerate(pieces) for c in range(p.shape[1] // width)]

    def kernel(slots, *refs):
        outs = refs[len(pieces) :]
        for q in range(4):
            for slot in range(4):

                @pl.when(slots[q] == slot)
                def _(q=q, slot=slot):
                    n, c = homes[slot]
                    at = slice((q % 2) * width, (q % 2 + 1) * width)
                    outs[q // 2][:, at] = refs[n][:, c * width : (c + 1) * width]

    return pl.pallas_call(
        ordered_after_scalars(kernel, len(pieces), len(behind)),
        grid_spec=pltpu.PrefetchScalarGridSpec(
            num_scalar_prefetch=1,
            grid=(rows // block,),
            in_specs=[pl.BlockSpec((block, p.shape[1]), lambda i, *_: (i, 0)) for p in pieces]
            + [ANY] * len(behind),
            out_specs=[pl.BlockSpec((block, 2 * width), lambda i, *_: (i, 0))] * 2,
        ),
        out_shape=[jax.ShapeDtypeStruct((rows, 2 * width), BF)] * 2,
        compiler_params=params(),
        cost_estimate=cost(rows, 16 * rows * width),
        name="split_terms",
    )(plan.slots, *pieces, *behind)


def ordered_after_scalars(kernel, count, extra):
    def run(scalars, *refs):
        kernel(scalars, *refs[:count], *refs[count + extra :])

    return run


def branch_terms(plan, attended, pieces, behind):
    rows = attended.shape[0]
    width = sum(p.shape[1] for p in pieces) // 4
    block = 256
    homes = [(n, c) for n, p in enumerate(pieces) for c in range(p.shape[1] // width)]

    def kernel(slots, att_ref, *refs):
        outs = refs[len(pieces) :]
        for q in range(4):
            for slot in range(4):

                @pl.when(slots[q] == slot)
                def _(q=q, slot=slot):
                    n, c = homes[slot]
                    at = slice((q % 2) * width, (q % 2 + 1) * width)
                    product = nn(att_ref[...], refs[n][:, c * width : (c + 1) * width])
                    outs[q // 2][:, at] = product.astype(BF)

    return pl.pallas_call(
        ordered_after_scalars(kernel, 1 + len(pieces), len(behind)),
        grid_spec=pltpu.PrefetchScalarGridSpec(
            num_scalar_prefetch=1,
            grid=(rows // block,),
            in_specs=[pl.BlockSpec((block, attended.shape[1]), lambda i, *_: (i, 0))]
            + [pl.BlockSpec(p.shape, lambda i, *_: (0, 0)) for p in pieces]
            + [ANY] * len(behind),
            out_specs=[pl.BlockSpec((block, 2 * width), lambda i, *_: (i, 0))] * 2,
        ),
        out_shape=[jax.ShapeDtypeStruct((rows, 2 * width), BF)] * 2,
        compiler_params=params(),
        cost_estimate=cost(0, 0),
        name="branch_terms",
    )(plan.slots, attended, *pieces, *behind)


def outer(left, right, slots, axis, folded, behind):
    rows = left.shape[0]
    if axis == 0:
        width, wide = left.shape[1] // 4, right.shape[1]
        in_specs = [
            pl.BlockSpec((rows, width), lambda i, slots: (0, slots[i])),
            pl.BlockSpec((rows, wide), lambda i, slots: (0, 0)),
        ]
    else:
        width, wide = left.shape[1], right.shape[1] // 4
        in_specs = [
            pl.BlockSpec((rows, width), lambda i, slots: (0, 0)),
            pl.BlockSpec((rows, wide), lambda i, slots: (0, slots[i])),
        ]
    beside = folded or axis == 1
    shape = (width, 2 * wide) if beside else (2 * width, wide)

    def first(i, slots):
        at = jnp.minimum(i, 1)
        return (0, at) if beside else (at, 0)

    def last(i, slots):
        at = jnp.maximum(i - 2, 0)
        return (0, at) if beside else (at, 0)

    def kernel(slots_ref, left_ref, right_ref, first_ref, last_ref):
        made = tn(left_ref[...], right_ref[...]).astype(BF)

        @pl.when(pl.program_id(0) < 2)
        def _():
            first_ref[...] = made

        @pl.when(pl.program_id(0) >= 2)
        def _():
            last_ref[...] = made

    return pl.pallas_call(
        ordered_after_scalars(kernel, 2, len(behind)),
        grid_spec=pltpu.PrefetchScalarGridSpec(
            num_scalar_prefetch=1,
            grid=(4,),
            in_specs=in_specs + [ANY] * len(behind),
            out_specs=[pl.BlockSpec((width, wide), first), pl.BlockSpec((width, wide), last)],
        ),
        out_shape=[jax.ShapeDtypeStruct(shape, BF)] * 2,
        compiler_params=params(),
        cost_estimate=cost(4 * rows * shape[0] * shape[1], 8 * 2**20),
        name="outer",
    )(slots, left, right, *behind)


def rows_spec(block, columns, first=0):
    return pl.BlockSpec((block, columns), lambda i, *_: (first // block + i, 0))


STEPS = 2


def part_shape(arrays, part):
    return (part.rows, arrays[0].shape[1]) if part is not None else arrays[0].shape


def enter(plan, part, ready, behind):
    arrays, specs = [], []
    if part is not None:
        arrays += [part.grad.own, part.grad.sent]
    if ready is not None:
        arrays += [ready.pair, ready.got]
    rows, columns = part_shape(arrays, part)
    block = rows // STEPS
    for n, array in enumerate(arrays):
        first = part.first if part is not None and n < 2 else 0
        specs.append(rows_spec(block, columns, first))

    def kernel(ends, *refs):
        given, results = refs[: len(arrays)], refs[len(arrays) :]
        sums = [
            (given[n][...].astype(F32) + given[n + 1][...].astype(F32)).astype(BF)
            for n in range(0, len(arrays), 2)
        ]
        results[0][...] = sums[0]
        if len(sums) == 2:
            results[1][...] = jnp.where(ends[0] != 0, sums[0], sums[1])

    count = len(arrays) // 2
    made = pl.pallas_call(
        ordered_after_scalars(kernel, len(arrays), len(behind)),
        grid_spec=pltpu.PrefetchScalarGridSpec(
            num_scalar_prefetch=1,
            grid=(STEPS,),
            in_specs=specs + [ANY] * len(behind),
            out_specs=[rows_spec(block, columns)] * count,
        ),
        out_shape=[jax.ShapeDtypeStruct((rows, columns), BF)] * count,
        compiler_params=params(),
        cost_estimate=cost(rows * columns, 6 * rows * columns * count),
        name="enter",
    )(plan.ends, *arrays, *behind)
    return made if count == 2 else (made[0], made[0])


def leave(plan, outs, term, there, got, writes, behind):
    rows, columns = got.shape
    block = rows // STEPS
    args, specs, shapes, out_specs, alias = [got], [], [], [], {}
    if term is not None:
        args.append(term)
        shapes.append(jax.ShapeDtypeStruct((rows, columns), BF))
        out_specs.append(rows_spec(block, columns))
    if writes is not None:
        args.append(there)
    specs = [rows_spec(block, columns)] * len(args)
    reads = len(args)
    for name, shape, wide, row, column, _ in writes or []:
        if name in outs:
            alias[1 + len(args)] = len(shapes)
            args.append(outs[name])
            specs.append(ANY)
        shapes.append(jax.ShapeDtypeStruct(shape, F32))
        out_specs.append(
            pl.BlockSpec((block, wide), lambda i, *_, r=row // block, c=column // wide: (r + i, c))
        )
    given = len(args)

    def kernel(ends, *refs):
        results = list(refs[given + len(behind) :])
        arrived = refs[0][...]
        if term is not None:
            total = refs[1][...].astype(F32) + arrived.astype(F32)
            results.pop(0)[...] = total.astype(BF)
        if writes is not None:
            total = jnp.where(ends[0] != 0, arrived, refs[reads - 1][...]).astype(F32)
            for out, (_, _, _, _, _, takes) in zip(results, writes):
                done = 0
                for start, size in takes:
                    out[:, done : done + size] = total[:, start : start + size]
                    done += size

    made = pl.pallas_call(
        kernel,
        grid_spec=pltpu.PrefetchScalarGridSpec(
            num_scalar_prefetch=1,
            grid=(STEPS,),
            in_specs=specs + [ANY] * len(behind),
            out_specs=out_specs,
        ),
        out_shape=shapes,
        input_output_aliases=alias,
        compiler_params=params(),
        cost_estimate=cost(rows * columns, 10 * rows * columns),
        name="leave",
    )(plan.ends, *args, *behind)
    made = list(made)
    first = made[0]
    pair = made.pop(0) if term is not None else None
    for (name, *_), value in zip(writes or [], made):
        outs[name] = value
    return pair, first


def take(plan, blocks, axis, behind):
    part = blocks[0][0].shape[axis] // 2
    sizes = [size for _, size, _ in blocks]

    def kernel(half, *refs):
        out_ref = refs[-1]
        at = 0
        for ref, size in zip(refs, sizes):
            if axis == 0:
                out_ref[:, at : at + size] = ref[...]
            else:
                out_ref[at : at + size] = ref[...]
            at += size

    specs = []
    for _, size, first in blocks:
        if axis == 0:
            spec = pl.BlockSpec((part, size), lambda i, half, first=first: (half[0], first))
        else:
            spec = pl.BlockSpec((size, part), lambda i, half, first=first: (first, half[0]))
        specs.append(spec)
    shape = (part, sum(sizes)) if axis == 0 else (sum(sizes), part)
    return pl.pallas_call(
        ordered_after_scalars(kernel, len(blocks), len(behind)),
        grid_spec=pltpu.PrefetchScalarGridSpec(
            num_scalar_prefetch=1,
            grid=(1,),
            in_specs=specs + [ANY] * len(behind),
            out_specs=pl.BlockSpec(shape, lambda i, half: (0, 0)),
        ),
        out_shape=jax.ShapeDtypeStruct(shape, BF),
        compiler_params=params(),
        cost_estimate=cost(0, 4 * shape[0] * shape[1]),
        name="take",
    )(plan.half, *[array for array, _, _ in blocks], *behind)


def project(rows_in, sides, cos, sin, ids, behind):
    rows, depth = rows_in.shape
    block = ids.shape[2]
    arrays = [array for pieces, _ in sides for _, side in pieces for array in side]
    widths = [sum(array.shape[1] for array in pieces[0][1]) for pieces, _ in sides]

    def kernel(*refs):
        in_ref, cos_ref, sin_ref, ids_ref = refs[:4]
        weights = refs[4 : 4 + len(arrays)]
        results = refs[4 + len(arrays) :]
        below = jnp.broadcast_to(ids_ref[0].astype(F32), (ID_ROWS, block)).astype(BF)
        results[0][block:, :block] = below
        at = 0
        for (pieces, turned), wide, out_ref in zip(sides, widths, results):
            total = None
            for first, side in pieces:
                values = [weights[at + n][...] for n in range(len(side))]
                at += len(side)
                value = values[0] if len(values) == 1 else jnp.concatenate(values, axis=1)
                term = nn(in_ref[:, first : first + value.shape[0]], value)
                total = term if total is None else total + term
            turned_part = turn(total[:, :turned], cos_ref[...], sin_ref[...])
            out_ref[:block, :turned] = turned_part.astype(BF)
            if turned < wide:
                out_ref[:block, turned:] = total[:, turned:].astype(BF)

    def of_rows(columns):
        return pl.BlockSpec((block, columns), lambda i: (i, 0))

    args = [rows_in, cos, sin, ids] + arrays
    specs = [of_rows(depth), of_rows(128), of_rows(128)]
    specs.append(pl.BlockSpec((1, 1, block), lambda i: (i, 0, 0)))
    specs += [pl.BlockSpec(a.shape, lambda i: (0, 0)) for a in arrays]
    steps = rows // block
    shapes = [(block + ID_ROWS * (n == 0), wide) for n, wide in enumerate(widths)]
    return pl.pallas_call(
        ordered(kernel, len(args), len(behind)),
        grid=(steps,),
        in_specs=specs + [ANY] * len(behind),
        out_specs=[pl.BlockSpec(shape, lambda i: (i, 0)) for shape in shapes],
        out_shape=[jax.ShapeDtypeStruct((steps * r, wide), BF) for r, wide in shapes],
        compiler_params=params(),
        cost_estimate=cost(0, 0),
        name="project",
    )(*args, *behind)


def back_projected(sides, behind):
    rows = sides[0][0].shape[0]
    count = len(sides[0][1])
    block = 256
    args = [s[0] for s in sides] + [a for s in sides for piece in s[1] for a in piece]

    def kernel(*refs):
        given, outs = refs[: len(args)], refs[len(args) :]
        totals = [None] * count
        at = len(sides)
        for k, (_, pieces) in enumerate(sides):
            for n, piece in enumerate(pieces):
                first = 0
                for _ in piece:
                    weight = given[at][...]
                    at += 1
                    term = nt(given[k][:, first : first + weight.shape[1]], weight)
                    first += weight.shape[1]
                    totals[n] = term if totals[n] is None else totals[n] + term
        for out, total in zip(outs, totals):
            out[...] = total.astype(BF)

    def of_rows(columns):
        return pl.BlockSpec((block, columns), lambda i: (i, 0))

    specs = [of_rows(s[0].shape[1]) for s in sides]
    specs += [pl.BlockSpec(a.shape, lambda i: (0, 0)) for a in args[len(sides) :]]
    widths = [piece[0].shape[0] for piece in sides[0][1]]
    return pl.pallas_call(
        ordered(kernel, len(args), len(behind)),
        grid=(rows // block,),
        in_specs=specs + [ANY] * len(behind),
        out_specs=[of_rows(w) for w in widths],
        out_shape=[jax.ShapeDtypeStruct((rows, w), BF) for w in widths],
        compiler_params=params(),
        cost_estimate=cost(4 * rows * sum(widths) * 512, 8 * 2**20),
        name="back_projected",
    )(*args, *behind)


def heads_back(rows_in, pieces, behind):
    rows, depth = rows_in.shape
    wide = pieces[0].shape[0]
    block = 256

    def kernel(*refs):
        in_ref, out_ref = refs[0], refs[-1]
        at, total = 0, None
        for ref in refs[1:-1]:
            size = ref.shape[1]
            term = nt(in_ref[:, at : at + size], ref[...])
            total = term if total is None else total + term
            at += size
        out_ref[...] = total.astype(BF)

    return pl.pallas_call(
        ordered(kernel, 1 + len(pieces), len(behind)),
        grid=(rows // block,),
        in_specs=[pl.BlockSpec((block, depth), lambda i: (i, 0))]
        + [pl.BlockSpec(p.shape, lambda i: (0, 0)) for p in pieces]
        + [ANY] * len(behind),
        out_specs=pl.BlockSpec((block, wide), lambda i: (i, 0)),
        out_shape=jax.ShapeDtypeStruct((rows, wide), BF),
        compiler_params=params(),
        cost_estimate=cost(2 * rows * depth * wide, 6 * 2**20),
        name="heads_back",
    )(rows_in, *pieces, *behind)


class TensorGather:
    def __init__(self, part):
        self.part = part
        self.far = lax.ppermute(part, "tp", flip(4, 2))
        self.near = lax.ppermute(part, "tp", flip(4, 1))

    def settle(self, clock):
        self.near = clock.did(clock.now(self.near))

    def relay(self, clock):
        self.far = clock.now(self.far)
        clock.did(self.far)
        self.far_near = lax.ppermute(self.far, "tp", flip(4, 1))

    def held(self):
        return [self.part, self.near, self.far, self.far_near]


class TensorScatter:
    def __init__(self, keep, send):
        self.keep = keep
        self.width = keep.shape[1] // 2
        self.got = lax.ppermute(send, "tp", flip(4, 1))

    def cross(self, clock):
        self.got = clock.now(self.got)
        keep, got = self.keep[:, self.width :], self.got[:, self.width :]
        far = clock.did((keep.astype(F32) + got.astype(F32)).astype(BF))
        self.far = lax.ppermute(far, "tp", flip(4, 2))

    def total(self, clock):
        far = clock.now(self.far)
        own = self.keep[:, : self.width].astype(F32) + self.got[:, : self.width].astype(F32)
        return own + far.astype(F32)


def tensor_total(values):
    values = values + lax.ppermute(values, "tp", flip(4, 1))
    return values + lax.ppermute(values, "tp", flip(4, 2))


class Weight:
    def __init__(self, plan, blocks, axis):
        self.plan, self.blocks, self.axis = plan, blocks, axis

    def take(self, clock):
        axis = self.axis
        if not self.plan.pairs:
            sent = [
                lax.slice_in_dim(array, first * size, (first + 1) * size, axis=1 - axis)
                for array, size, first in self.blocks
            ]
            sent = jnp.concatenate(sent, axis=1 - axis)
            self.out = lax.all_gather(sent, "fsdp", axis=axis, tiled=True)
            return
        self.sent = clock.did(take(self.plan, self.blocks, axis, clock.last))

    def start(self, clock):
        if self.plan.pairs:
            self.near = lax.ppermute(clock.go(self.sent), "fsdp", flip(2, 1))

    def relay(self, clock):
        if self.plan.pairs:
            self.near = clock.did(clock.now(self.near))
            self.far = lax.ppermute(self.near, "ctx", flip(4, 1))

    def arrive(self, clock):
        if self.plan.pairs:
            self.far = clock.did(clock.now(self.far))

    def pieces(self, own):
        return [own, self.near, self.far] if self.plan.pairs else [self.out]


class Grad:
    def __init__(self, plan, clock, left, right, axis, folded=False):
        self.away, self.own = outer(left, right, plan.sides, axis, folded, clock.last)
        clock.did(self.away)
        self.sent = None
        self.arrived = False


class Part:
    def __init__(self, grad, first, rows, writes):
        self.grad, self.first, self.rows, self.writes = grad, first, rows, writes
        self.columns = grad.own.shape[1]
        self.landed = False


class Line:
    def __init__(self, plan, clock, outs):
        self.plan, self.clock, self.outs = plan, clock, outs
        self.waiting, self.crossing, self.sent = [], [], []
        self.leaving, self.flying, self.depth = [], [], 0

    def add(self, grad, parts):
        self.leaving.append(grad)
        self.waiting += [Part(grad, *part) for part in parts]
        self.kick()

    def kick(self):
        while self.leaving and len(self.flying) < self.depth:
            grad = self.leaving.pop(0)
            grad.sent = lax.ppermute(self.clock.go(grad.away), "fsdp", flip(2, 1))
            self.flying.append(grad)

    def step(self):
        plan, clock = self.plan, self.clock
        part = self.waiting.pop(0) if self.waiting else None
        if part is not None and not part.grad.arrived:
            grad = part.grad
            grad.sent = clock.did(clock.now(grad.sent))
            grad.arrived = True
            self.flying.remove(grad)
            self.kick()
        ready = None
        if len(self.crossing) > (1 if part is not None else 0):
            ready = self.crossing.pop(0)
        swaps = [(part, ready)]
        if part is not None and ready is not None and part.columns != ready.columns:
            swaps = [(None, ready), (part, None)]
        sent = []
        for one, other in swaps if part is not None or ready is not None else []:
            term, there = enter(plan, one, other, clock.last)
            clock.did(there)
            got = lax.ppermute(there, "ctx", flip(4, 1))
            sent.append((one, term if one is not None else None, there, got, other))
        self.sent.append(sent)
        if len(self.sent) > 1 or not sent:
            for part, term, there, got, ready in self.sent.pop(0):
                writes = ready.writes if ready is not None else None
                pair, made = leave(plan, self.outs, term, there, got, writes, clock.last)
                clock.did(made)
                if part is not None:
                    part.pair = pair
                    part.got = lax.ppermute(pair, "ctx", [(1, 2), (2, 1)])
                    self.crossing.append(part)
        for part in self.crossing[:-1]:
            if not part.landed:
                part.got = clock.did(clock.now(part.got))
                part.landed = True
        if self.sent and not self.sent[0]:
            self.sent.pop(0)

    def drain(self):
        while self.waiting or self.crossing or self.sent:
            self.step()


def earlier_blocks(rows):
    return [rows] + [
        lax.ppermute(rows, "ctx", [(i, i + k) for i in range(4 - k)]) for k in range(1, 4)
    ]


def on_device(
    tokens,
    segment_ids,
    positions,
    attn_gain,
    w_query,
    w_key,
    w_value,
    w_output,
    mlp_gain,
    w_gate,
    w_up,
    w_down,
    cotangent,
):
    plan = Plan()
    clock = Clock()
    outs = {}
    line = Line(plan, clock, outs)
    seqs, length, part_width = tokens.shape
    rows = seqs * length
    width = part_width * plan.tp
    quarter = width // 4
    kv_width = w_key.shape[1]
    heads_width = w_query.shape[1]
    hidden = w_gate.shape[1]
    span = hidden // SPLITS
    tile = span // 2
    half = hidden // 2
    token_rows = tokens.reshape(rows, part_width)
    cot_rows = cotangent.reshape(rows, part_width)

    kv_weight = Weight(plan, [(w_key, kv_width, 0), (w_value, kv_width, 0)], 0)
    q_weight = Weight(plan, [(w_query, heads_width, 0)], 0)
    o_weight = Weight(plan, [(w_output, heads_width, 0)], 1)
    gu_weights = [
        Weight(plan, [(w, tile, 2 * j + i) for i in range(2) for w in (w_gate, w_up)], 0)
        for j in range(SPLITS)
    ]
    down_weights = [Weight(plan, [(w_down, half, h)], 1) for h in range(2)]
    token_part = TensorGather(with_gain(token_rows, attn_gain))
    kv_weight.take(clock)
    kv_weight.start(clock)
    q_weight.take(clock)
    q_weight.start(clock)
    token_part.settle(clock)
    kv_weight.relay(clock)
    o_weight.take(clock)
    frequency = jnp.exp(jnp.arange(HD // 2, dtype=F32) * (-2.0 * math.log(THETA) / HD))
    turn_angle = positions.reshape(rows, 1).astype(F32) * frequency
    cos_half, sin_half = jnp.cos(turn_angle), jnp.sin(turn_angle)
    cos = after(jnp.concatenate([cos_half] * 4, axis=1))
    sin = after(jnp.concatenate([-sin_half, sin_half] * 2, axis=1))
    token_part.relay(clock)
    q_weight.relay(clock)
    o_weight.start(clock)
    gu_weights[0].take(clock)
    gu_weights[0].start(clock)
    normed, scale_attn = lay_norm(plan, token_part.held(), clock.last)
    scale_attn = scale_attn[:, :1]
    clock.did(normed)
    kv_weight.arrive(clock)
    q_weight.arrive(clock)

    def stack(weight, own):
        at, pieces = 0, []
        for piece in weight.pieces(own):
            side = piece if isinstance(piece, list) else [piece]
            pieces.append((at, side))
            at += side[0].shape[0]
        return pieces

    kv_pieces = stack(kv_weight, [w_key, w_value])
    q_pieces = stack(q_weight, w_query)
    segq = segment_ids[:, None, :]
    kv_own, query_rot = project(
        normed, [(kv_pieces, kv_width), (q_pieces, heads_width)], cos, sin, segq, clock.last
    )
    clock.did(kv_own)
    segq = segq.astype(F32)
    kv_blocks = earlier_blocks(kv_own.reshape(seqs, length + ID_ROWS, 2 * kv_width))
    cot_part = TensorGather(clock.go(cot_rows))
    cot_part.settle(clock)
    gu_weights[1].take(clock)
    o_weight.relay(clock)
    gu_weights[1].start(clock)
    gu_weights[2].take(clock)
    gu_weights[3].take(clock)
    for n in range(1, 4):
        kv_blocks[n] = clock.did(clock.now(kv_blocks[n]))
    cot_part.relay(clock)
    attended, log_totals = attend_forward(query_rot, kv_blocks, segq, clock.last)
    clock.did(attended)
    o_weight.arrive(clock)
    o_pieces = o_weight.pieces(w_output)
    keep, away = branch_terms(plan, attended, o_pieces, clock.last)
    clock.did(away)
    mid_branch = TensorScatter(keep, away)
    mid_branch.cross(clock)
    gu_weights[0].relay(clock)
    gu_weights[2].start(clock)
    cot_all = clock.did(lay(plan, cot_part.held(), clock.last))
    gu_weights[1].relay(clock)
    gu_weights[3].start(clock)
    resid_mid = token_rows.astype(F32) + mid_branch.total(clock)
    gained_part = TensorGather(clock.did((resid_mid * mlp_gain).astype(BF)))
    gained_part.settle(clock)
    for w in down_weights:
        w.take(clock)
    gu_weights[0].arrive(clock)
    gained_part.relay(clock)
    square_sum = clock.go(jnp.sum(resid_mid * resid_mid, axis=-1))
    got = lax.ppermute(square_sum, "tp", flip(4, 1))
    gu_weights[2].relay(clock)
    down_weights[0].start(clock)
    square_sum = clock.did(square_sum + clock.now(got))
    got = lax.ppermute(square_sum, "tp", flip(4, 2))
    gained = clock.did(lay(plan, gained_part.held(), clock.last))
    square_sum = clock.did(square_sum + clock.now(got))
    scale_mlp = lax.rsqrt(square_sum / width + EPS)[:, None]

    def gu_segments(j):
        def at_block(i):
            return (2 * i, 2 * i + 1)

        weight = gu_weights[j]
        if not plan.pairs:
            return [(0, width, (weight.out, weight.out), at_block)]
        return [
            (0, 2 * quarter, (w_gate, w_up), lambda i: (2 * j + i, 2 * j + i)),
            (2 * quarter, quarter, (weight.near, weight.near), at_block),
            (3 * quarter, quarter, (weight.far, weight.far), at_block),
        ]

    per = SPLITS // 2

    def down_segments(j):
        weight = down_weights[j // per]

        def at_block(i):
            return 2 * (j % per) + i

        if not plan.pairs:
            return [(0, width, weight.out, at_block)]
        return [
            (0, 2 * quarter, w_down, lambda i: 2 * j + i),
            (2 * quarter, quarter, weight.near, at_block),
            (3 * quarter, quarter, weight.far, at_block),
        ]

    def finish(left, right, axis, parts):
        total = lax.psum_scatter(tn(left, right), "fsdp", scatter_dimension=axis, tiled=True)
        total = lax.psum(total, "ctx")
        for first, count, writes in parts:
            for name, shape, _, row, column, takes in writes:
                value = jnp.concatenate(
                    [total[first : first + count, at : at + size] for at, size in takes], axis=1
                )
                base = outs[name] if name in outs else jnp.zeros(shape, F32)
                outs[name] = place(base, value, row, column)

    def send(left, right, axis, parts, folded=False):
        if plan.pairs:
            line.add(Grad(plan, clock, left, right, axis, folded), parts)
        else:
            finish(left, right, axis, parts)

    raws, acts = [], []
    line.depth = 2
    for j in range(SPLITS):
        if j > 0:
            gu_weights[j].arrive(clock)
        raw, act = gate_up(j, gained, scale_mlp, gu_segments(j), span, clock.last)
        raws.append(raw)
        acts.append(clock.did(act))
        own = w_down.shape[1]
        writes = [("down", w_down.shape, own, j * span, 0, [(0, own)])]
        send(act, cot_all, 1, [(0, span, writes)])
        if j == 0:
            gu_weights[3].relay(clock)
            down_weights[1].start(clock)
        if j == 1:
            down_weights[0].relay(clock)
        if j == 2:
            down_weights[1].relay(clock)
    down_weights[0].arrive(clock)
    gu_grads, inners = [], []

    def send_gu(j):
        share = w_gate.shape[0] // 2
        takes = [[(2 * i * tile + side * tile, tile) for i in range(2)] for side in range(2)]
        parts = []
        for r in range(2):
            writes = [
                (name, w_gate.shape, span, r * share, j * span, way)
                for name, way in zip(("gate", "up"), takes)
            ]
            parts.append((r * share, share, writes))
        send(gained, gu_grads[j], 0, parts)

    for j in range(SPLITS):
        if j == per:
            down_weights[1].arrive(clock)
        gu_grad, inner = gate_up_back(
            j, cot_all, scale_mlp, raws[j], down_segments(j), span, clock.last
        )
        clock.did(gu_grad)
        gu_grads.append(gu_grad)
        inners.append(inner)
        if j % 2 == 1:
            line.step()
    mid_inner = tensor_total(jnp.sum(sum(inners), axis=1))[:, None]
    send_gu(0)
    if plan.pairs:
        near = [w.near for w in gu_weights]
        far = [w.far for w in gu_weights]
        terms = back_to_width(gu_grads, w_gate, w_up, near, far, span, clock.last)
    else:
        terms = [sum(nt(clock.now(g), w.out) for g, w in zip(gu_grads, gu_weights)).astype(BF)]
    clock.did(terms[0])
    line.step()
    keep, away = split_terms(plan, terms, clock.last)
    clock.did(away)
    mid_scatter = TensorScatter(keep, away)
    mid_inner = clock.did(clock.now(mid_inner))
    send_gu(1)
    mid_scatter.cross(clock)
    line.step()
    send_gu(2)
    scaled_grad = mid_scatter.total(clock)
    mlp_gain_part = jnp.sum(scaled_grad * resid_mid, axis=0)
    resid_mid_grad = (
        cot_rows.astype(F32)
        + mlp_gain * scaled_grad
        - resid_mid * (scale_mlp * scale_mlp * mid_inner / width)
    )
    branch_part = TensorGather(clock.did(resid_mid_grad.astype(BF)))
    branch_part.settle(clock)
    line.step()
    send_gu(3)
    branch_part.relay(clock)
    branch_grad = clock.did(lay(plan, branch_part.held(), clock.last))

    attended_grad = clock.did(heads_back(branch_grad, o_pieces, clock.last))
    line.step()
    query_grad, in_inner, *kv_terms = attend_backward(
        query_rot, attended_grad, attended, log_totals, cos, sin, kv_blocks, segq, clock.last
    )
    clock.did(query_grad)

    def hop(terms):
        return lax.ppermute(terms.astype(BF), "ctx", [(i, i - 1) for i in range(1, 4)])

    hopping = hop(kv_terms[3])
    line.step()
    line.step()
    shape = w_output.shape
    send(
        attended, branch_grad, 1,
        [(0, shape[0], [("output", shape, shape[1], 0, 0, [(0, shape[1])])])],
    )
    hopping = hop(kv_terms[2].astype(F32) + clock.did(clock.now(hopping)).astype(F32))
    line.step()

    def halves(name, array, columns, at, total):
        share, wide = array.shape[0] // 2, array.shape[1]
        if not plan.pairs:
            return [(name, array.shape, wide, 0, 0, [(at, wide)])]
        return [
            (name + str(r), (share, wide), wide, 0, 0, [(r * total + at, wide)]) for r in range(2)
        ]

    count = quarter if plan.pairs else w_query.shape[0]
    writes = halves("query", w_query, heads_width, 0, heads_width)
    send(normed, query_grad, 0, [(0, count, writes)], folded=True)
    hopping = hop(kv_terms[1].astype(F32) + clock.did(clock.now(hopping)).astype(F32))
    if plan.pairs:
        near = [w.near for w in down_weights]
        far = [w.far for w in down_weights]
        terms = down(acts, w_down, near, far, span, clock.last)
    else:
        terms = 0.0
        for j in range(SPLITS):
            at = slice((j % per) * span, (j % per + 1) * span)
            terms = terms + nn(acts[j], down_weights[j // per].out[at])
        terms = [terms.astype(BF)]
    clock.did(terms[0])
    line.step()
    kv_sum = kv_terms[0] + clock.did(clock.now(hopping)).astype(F32)
    own = kv_own.reshape(seqs, length + ID_ROWS, 2 * kv_width)[:, :length]
    kv_inner = jnp.sum(kv_sum * own.astype(F32), axis=2).reshape(rows)
    kv_sum = kv_sum.reshape(rows, 2 * kv_width)
    kv_grad = clock.did(turn_rows(kv_sum, cos, -sin, kv_width))
    in_inner = jnp.sum(in_inner, axis=1) + kv_inner
    in_inner = tensor_total(in_inner)[:, None]
    writes = halves("key", w_key, kv_width, 0, 2 * kv_width)
    writes += halves("value", w_value, kv_width, kv_width, 2 * kv_width)
    send(normed, kv_grad, 0, [(0, count, writes)], folded=True)
    line.step()
    sides = [
        (grads, [side for _, side in pieces])
        for grads, pieces in ((query_grad, q_pieces), (kv_grad, kv_pieces))
    ]
    in_sides = back_projected(sides, clock.last)
    clock.did(in_sides[0])
    keep, away = split_terms(plan, in_sides, clock.last)
    clock.did(away)
    in_scatter = TensorScatter(keep, away)
    in_inner = clock.did(clock.now(in_inner))
    line.step()
    in_scatter.cross(clock)
    keep, away = split_terms(plan, terms, clock.last)
    clock.did(away)
    out_scatter = TensorScatter(keep, away)
    line.step()
    normed_grad = in_scatter.total(clock)
    own_tokens = token_rows.astype(F32)
    attn_gain_part = jnp.sum(normed_grad * own_tokens * scale_attn, axis=0)
    input_grad = clock.did(
        resid_mid_grad
        + scale_attn * attn_gain * normed_grad
        - own_tokens * (scale_attn * scale_attn * in_inner / width)
    )
    out_scatter.cross(clock)
    line.step()
    gain_grads = clock.now(jnp.concatenate([attn_gain_part, mlp_gain_part]))
    if plan.pairs:
        got = lax.ppermute(gain_grads, "fsdp", flip(2, 1))
        output = clock.did((resid_mid + out_scatter.total(clock)).astype(BF))
        gain_grads = clock.did(gain_grads + clock.now(got))
        line.step()
        for bits in (1, 3):
            got = lax.ppermute(gain_grads, "ctx", flip(4, bits))
            line.step()
            gain_grads = clock.did(gain_grads + clock.now(got))
    else:
        output = (resid_mid + out_scatter.total(clock)).astype(BF)
        gain_grads = lax.psum(gain_grads, ("fsdp", "ctx"))
    line.drain()

    def joined(name):
        return jnp.concatenate([outs[name + "0"], outs[name + "1"]]) if plan.pairs else outs[name]

    shape = (seqs, length, part_width)
    return (
        output.reshape(shape),
        input_grad.reshape(shape),
        gain_grads[:part_width],
        joined("query"),
        joined("key"),
        joined("value"),
        outs["output"],
        gain_grads[part_width:],
        outs["gate"],
        outs["up"],
        outs["down"],
    )


def solution(mesh):
    rows = P("fsdp", "ctx", "tp")
    per_token = P("fsdp", "ctx")
    columns = P("fsdp", "tp")
    across = P("tp", "fsdp")
    gain = P("tp")
    return jax.shard_map(
        on_device,
        mesh=mesh,
        in_specs=(
            rows, per_token, per_token, gain, columns, columns, columns, across, gain,
            columns, columns, across, rows,
        ),
        out_specs=(
            rows, rows, gain, columns, columns, columns, across, gain, columns, columns, across,
        ),
        check_vma=False,
    )
```
